512 devices in a mesh: ctx: 64 (over z, x, core), head: 8 (over y).
Axes of the slice: x: 4, y: 8, z: 8, core: 2. Of those that a mesh axis runs over, the one named last changes fastest.
Arguments:
- hidden: bfloat16 [2, 4, 16384], P(None, None, 'ctx'), may hold values from -400 to 400
- norm_gain: bfloat16 [16384], P('ctx'), may hold values from 0.099609375 to 1.8984375
- w_query: bfloat16 [16384, 16384], P('ctx', 'head'), may hold values from -0.046875 to 0.046875
- w_keyval: bfloat16 [16384, 2048], P('ctx', 'head'), may hold values from -0.046875 to 0.046875
- w_out: bfloat16 [16384, 16384], P('head', 'ctx'), may hold values from -6 to 6
- cache: bfloat16 [2048, 128, 8, 256], P('ctx', None, 'head'), may hold values from -240 to 240
- page_table: int32 [4, 256], replicated, may hold values from -1 to 2047, as said below
- lengths: int32 [4], replicated, may hold values from 16384 to 32768, as said below
- owners: int32 [4], replicated, may hold values from 0 to 63, as said below
Outputs:
- delivered: bfloat16 [64, 2, 16384], P('ctx')
The draws below stay inside these ranges and needn't reach their ends.
Inputs may be any that keep to these rules, and one draw needn't show every extreme that they name: `page_table`: entries of one table are distinct page numbers or -1; entry k of request b is a page number exactly when k < ceil(lengths[b] / 128). One index of ctx holds up to 32 used pages, and the used pages lie unevenly over ctx. `lengths`: some request has exactly 32768 cached tokens. `owners`: distinct slots.
All inputs are finite; a program needn't handle non-finite values.
Results may differ from the reference program's by a relative error of at most 0.022.
The reference program's roundings to bfloat16 on the way (of `normed`, `attended` and `projected`) count: a program that leaves them out, or rounds other values in their place, can miss the bound.
Values may be sent and summed in bfloat16 or wider, within the bound.
No kernel may reach another device: no remote copies, remote signals or barrier semaphores. Data moves between devices by JAX's collectives and lax.ppermute only.
A program may use at most 64 MiB of HBM per device.

```python
import math
import jax
import jax.numpy as jnp
from jax import lax

D = 16384
QH = 128
KVH = 8
HD = 128
REQS = 4
STEPS = 2
PAGE = 128
PAGES_DEV = 32
POOL = 2048
MAXP = 256
SLOTS = 64


def page_layout(key):
    key_len, key_top, key_rank, key_mix = jax.random.split(jax.random.fold_in(key, 11), 4)
    longest_len = MAXP * PAGE
    lengths_drawn = jax.random.randint(key_len, (REQS,), longest_len // 2, longest_len + 1)
    longest = jax.random.randint(key_top, (), 0, REQS)
    shortest = (longest + 1) % REQS
    lengths_drawn = jnp.where(jnp.arange(REQS) == shortest, longest_len // 2, lengths_drawn)
    lengths_drawn = jnp.where(jnp.arange(REQS) == longest, longest_len, lengths_drawn)
    counts = (lengths_drawn + PAGE - 1) // PAGE
    used_pages = jnp.sum(counts)
    page_ids = jnp.arange(POOL)
    device_of = page_ids // PAGES_DEV
    score = jax.random.randint(key_rank, (POOL,), 0, POOL) + device_of * (2 * PAGES_DEV)
    score = jnp.where(page_ids == POOL - 1, -1, score)
    ranking = jnp.argsort(score, stable=True)
    position = jnp.arange(POOL)
    shuffle_key = jnp.where(position < used_pages, jax.random.randint(key_mix, (POOL,), 0, POOL), POOL + position)
    ranking = ranking[jnp.argsort(shuffle_key, stable=True)]
    starts = jnp.cumsum(counts) - counts
    column = jnp.arange(MAXP)
    entries = jnp.minimum(starts[:, None] + column[None, :], POOL - 1)
    table_out = jnp.where(column[None, :] < counts[:, None], ranking[entries], -1)
    return (table_out.astype(jnp.int32), lengths_drawn.astype(jnp.int32))


def draw_page_table(key, part):
    return page_layout(key)[0]


def draw_lengths(key, part):
    return page_layout(key)[1]


def draw_owners(key, part):
    key = jax.random.fold_in(key, 5)
    key_perm, key_place = jax.random.split(key)
    others = jax.random.permutation(key_perm, SLOTS - 1)[:REQS - 1]
    joined = jnp.concatenate([others, jnp.array([SLOTS - 1], dtype=others.dtype)])
    return jax.random.permutation(key_place, joined).astype(jnp.int32)


def draw_cache(key, part):
    key = jax.random.fold_in(key, 7)
    key_base = jax.random.fold_in(key, 0)
    key_dir = jax.random.fold_in(key, 3)
    key_lift = jax.random.fold_in(key, 4)
    base_draw = jnp.clip(jax.random.normal(key_base, (POOL, PAGE, KVH, 2 * HD), jnp.float32), -6.0, 6.0)
    direction = jnp.clip(jax.random.normal(key_dir, (1, 1, KVH, HD), jnp.float32), -3.0, 3.0)
    lift = jax.random.uniform(key_lift, (POOL, 1, KVH, 1), jnp.float32, 0.0, 16.0)
    keys_part = base_draw[..., :HD]
    values_part = base_draw[..., HD:]
    keys_part = keys_part + lift * direction
    return jnp.concatenate([keys_part, values_part], axis=-1).astype(jnp.bfloat16)


def draw_hidden(key, part):
    key = jax.random.fold_in(key, 3)
    key_col, key_row, key_base = jax.random.split(key, 3)
    column_scale = jnp.exp(jax.random.uniform(key_col, (D,), jnp.float32, 0.0, math.log(10.0)))
    column_scale = column_scale * 3.0 ** (jnp.arange(D, dtype=jnp.float32) / D) / 4.0
    row_scale = jnp.exp(jax.random.uniform(key_row, (STEPS, REQS, 1), jnp.float32, 0.0, math.log(10.0)))
    base_draw = jnp.clip(jax.random.normal(key_base, (STEPS, REQS, D), jnp.float32), -5.0, 5.0)
    return (base_draw * row_scale * column_scale).astype(jnp.bfloat16)


def level_of(key, shape, pieces, least, top_value):
    loudness, own = 1.0, jax.random.fold_in(key, 6)
    for dim, blocks in pieces:
        draws = jnp.exp(jax.random.uniform(jax.random.fold_in(own, dim), (blocks,), jnp.float32, least / len(pieces), top_value / len(pieces)))
        loudness = loudness * jnp.repeat(draws, shape[dim] // blocks).reshape([-1 if axis == dim else 1 for axis in range(len(shape))])
    return loudness


def gaussian(own_key, shape, scale, limit, cuts=(), kind=jnp.bfloat16):
    level = level_of(own_key, shape, cuts, -0.22, 0.18) if cuts else 1.0
    result = jax.random.normal(own_key, shape, jnp.float32) * scale * level
    return jnp.minimum(jnp.maximum(result, -limit), limit).astype(kind)


def setup_inputs(seed: int = 0) -> dict:
    streams_of = jax.random.split(jax.random.key(seed), 10)
    hidden = draw_hidden(jax.random.fold_in(streams_of[9], 71), 0)
    norm_gain = jnp.clip(1.0 + 0.18 * jax.random.normal(streams_of[1], (D,), jnp.float32), 0.099609375, 1.8984375).astype(jnp.bfloat16)
    w_query = gaussian(streams_of[2], (D, QH * HD), D ** -0.5, 0.046875, ((0, 64), (1, 8)))
    w_keyval = gaussian(streams_of[3], (D, KVH * 2 * HD), D ** -0.5, 0.046875, ((0, 64), (1, 8)))
    w_out = gaussian(streams_of[4], (QH * HD, D), (max(1, QH * HD // (MAXP * PAGE))) ** -0.5, 6.0, ((0, 8), (1, 64)))
    cache = draw_cache(jax.random.fold_in(streams_of[9], 71), 0)
    page_table = draw_page_table(jax.random.fold_in(streams_of[9], 71), 0)
    lengths = draw_lengths(jax.random.fold_in(streams_of[9], 71), 0)
    owners = draw_owners(jax.random.fold_in(streams_of[9], 71), 0)
    return {"hidden": hidden, "norm_gain": norm_gain, "w_query": w_query, "w_keyval": w_keyval, "w_out": w_out, "cache": cache, "page_table": page_table, "lengths": lengths, "owners": owners}


def frequencies(head_size):
    halfway = head_size // 2
    inverse = 500000.0 ** (-(jnp.arange(halfway, dtype=jnp.float32) * 2.0 / head_size))
    wavelength = 2.0 * math.pi / inverse
    smooth = (8192.0 / wavelength - 1.0) / 3.0
    blended = (1.0 - smooth) * inverse / 8.0 + smooth * inverse
    return jnp.where(wavelength < 2048.0, inverse, jnp.where(wavelength > 8192.0, inverse / 8.0, blended))

def rotate(vector, position):
    halfway = vector.shape[-1] // 2
    inverse = frequencies(vector.shape[-1])
    angles = position[..., None] * inverse
    angles = jnp.concatenate([angles, angles], axis=-1)
    turned = jnp.concatenate([-vector[..., halfway:], vector[..., :halfway]], axis=-1)
    return vector * jnp.cos(angles) + turned * jnp.sin(angles)

def reference(hidden, norm_gain, w_query, w_keyval, w_out, cache, page_table, lengths, owners):
    group_size = QH // KVH
    hidden_f = hidden.astype(jnp.float32)
    mean_square = lax.optimization_barrier(jnp.mean(hidden_f * hidden_f, axis=-1, keepdims=True))
    normed = (hidden_f * norm_gain.astype(jnp.float32) * lax.rsqrt(mean_square + 1e-05)).astype(jnp.bfloat16)
    flattened = normed.reshape(STEPS * REQS, D)
    raw_query = jnp.dot(flattened, w_query, preferred_element_type=jnp.float32).reshape(STEPS, REQS, KVH, group_size, HD)
    key_value = jnp.dot(flattened, w_keyval, preferred_element_type=jnp.float32).reshape(STEPS, REQS, KVH, 2 * HD)
    position = (lengths[None, :] + jnp.arange(STEPS, dtype=jnp.int32)[:, None]).astype(jnp.float32)
    queries = rotate(raw_query, position[:, :, None, None]).astype(jnp.bfloat16)
    new_keys = rotate(key_value[..., :HD], position[:, :, None]).astype(jnp.bfloat16)
    new_values = key_value[..., HD:].astype(jnp.bfloat16)
    softmax_scale = HD ** (-0.5)
    causal = jnp.arange(STEPS)[None, :] <= jnp.arange(STEPS)[:, None]

    def one_request(items):
        table_row, length, query_b, key_new, value_new = items
        pages = cache[jnp.maximum(table_row, 0)].reshape(MAXP * PAGE, KVH, 2 * HD)
        keys_b = pages[..., :HD].astype(jnp.float32)
        values_b = pages[..., HD:].astype(jnp.float32)
        valid = jnp.arange(MAXP * PAGE, dtype=jnp.int32) < length
        query_f = query_b.astype(jnp.float32)
        scores = jnp.einsum('skgd,tkd->skgt', query_f, keys_b) * softmax_scale
        scores = jnp.where(valid[None, None, None, :], scores, -jnp.inf)
        new_scores = jnp.einsum('skgd,tkd->skgt', query_f, key_new.astype(jnp.float32)) * softmax_scale
        new_scores = jnp.where(causal[:, None, None, :], new_scores, -jnp.inf)
        row_max = jnp.maximum(lax.optimization_barrier(jnp.max(scores, axis=-1)), lax.optimization_barrier(jnp.max(new_scores, axis=-1)))
        weights = jnp.exp(scores - row_max[..., None])
        new_weights = jnp.exp(new_scores - row_max[..., None])
        totals = lax.optimization_barrier(jnp.sum(weights, axis=-1)) + lax.optimization_barrier(jnp.sum(new_weights, axis=-1))
        weighted = jnp.einsum('skgt,tkd->skgd', weights.astype(jnp.bfloat16).astype(jnp.float32), values_b)
        weighted = weighted + jnp.einsum('skgt,tkd->skgd', new_weights.astype(jnp.bfloat16).astype(jnp.float32), value_new.astype(jnp.float32))
        attended = weighted / totals[..., None]
        return attended.reshape(STEPS, QH * HD).astype(jnp.bfloat16)
    stacked = lax.map(one_request, (page_table, lengths, jnp.transpose(queries, (1, 0, 2, 3, 4)), jnp.transpose(new_keys, (1, 0, 2, 3)), jnp.transpose(new_values, (1, 0, 2, 3))))
    attended = jnp.transpose(stacked, (1, 0, 2)).reshape(STEPS * REQS, QH * HD)
    projected = jnp.dot(attended, w_out, preferred_element_type=jnp.float32).astype(jnp.bfloat16).reshape(STEPS, REQS, D)
    onehot = (owners[:, None] == jnp.arange(SLOTS, dtype=jnp.int32)[None, :]).astype(jnp.float32)
    delivered = jnp.einsum('bc,sbd->csd', onehot, projected.astype(jnp.float32))
    return delivered.astype(jnp.bfloat16)
```

```python
import functools
import math

import jax
import jax.numpy as jnp
from jax import lax
from jax.experimental import pallas as pl
from jax.experimental.pallas import tpu as pltpu
from jax.sharding import PartitionSpec as P

HD = 128
HALF = HD // 2
EPSILON = 1e-05
NEGATIVE = -1e30
FLOOR = -1e29
F32 = jnp.float32
BF16 = jnp.bfloat16


def frequencies(head_size):
    halfway = head_size // 2
    inverse = 500000.0 ** (-(jnp.arange(halfway, dtype=F32) * 2.0 / head_size))
    wavelength = 2.0 * math.pi / inverse
    smooth = (8192.0 / wavelength - 1.0) / 3.0
    blended = (1.0 - smooth) * inverse / 8.0 + smooth * inverse
    return jnp.where(
        wavelength < 2048.0, inverse, jnp.where(wavelength > 8192.0, inverse / 8.0, blended)
    )


def iota(shape, dim):
    return lax.broadcasted_iota(jnp.int32, shape, dim)


def dot(a, b):
    return jnp.dot(a, b, preferred_element_type=F32)


def dot_t(a, b):
    return lax.dot_general(a, b, (((1,), (1,)), ((), ())), preferred_element_type=F32)


def call(kernel, out, scratch=(), n_in=1, smem=()):
    specs = [
        pl.BlockSpec(memory_space=pltpu.SMEM if i in smem else pltpu.VMEM) for i in range(n_in)
    ]
    return pl.pallas_call(
        kernel,
        out_shape=out,
        in_specs=specs,
        out_specs=pl.BlockSpec(memory_space=pltpu.VMEM),
        scratch_shapes=list(scratch),
        compiler_params=pltpu.CompilerParams(vmem_limit_bytes=32 * 1024 * 1024),
    )


def project_kernel(hidden_ref, gain_ref, wq_ref, wkv_ref, out_ref):
    gain = gain_ref[...].astype(F32)
    hid = [hidden_ref[s].astype(F32) for s in range(2)]
    width = hid[0].shape[1]
    row = iota((16, width), 0) % 4
    spread = [
        jnp.concatenate([h[b : b + 1] for b in range(4) for _ in range(4)], axis=0) for h in hid
    ]
    scaled = [x * gain for x in spread]

    def split(x):
        high = x.astype(BF16)
        return high, (x - high.astype(F32)).astype(BF16)

    zero = jnp.zeros_like(scaled[0])
    lhs_q = split(jnp.where(row == 0, scaled[0], jnp.where(row == 1, scaled[1], zero)))
    lhs_q = jnp.concatenate(lhs_q, axis=0)
    lhs_kv = [split(jnp.where(row == 2, x, zero)) for x in scaled]
    lhs_kv = jnp.concatenate([p for pair in lhs_kv for p in pair], axis=0)
    part_kv = dot(lhs_kv, wkv_ref[...])
    part_kv = [part_kv[0:16] + part_kv[16:32], part_kv[32:48] + part_kv[48:64]]
    squares = [jnp.sum(x * x, axis=-1, keepdims=True) for x in spread]
    tile_row = iota((16, HD), 0) % 4
    lane = iota((16, HD), 1)
    square = jnp.where(lane < HALF, squares[0], squares[1])
    square = jnp.where(tile_row == 3, square, 0.0)
    part_q = dot(lhs_q, wq_ref[...])
    part_q = part_q[0:16] + part_q[16:32]
    heads = part_q.shape[1] // HD
    for h in range(heads):
        block = part_q[:, h * HD : (h + 1) * HD] + square
        if h < 4:
            block = block + part_kv[h % 2][:, (h // 2) * HD : (h // 2 + 1) * HD]
        out_ref[h * 16 : (h + 1) * 16, :] = block


def finish_kernel(inverse_width, parts_ref, cos_ref, sin_ref, first_ref, out_ref):
    n = parts_ref.shape[0]
    total = parts_ref[0:8, :]
    for k in range(1, n // 8):
        total = total + parts_ref[k * 8 : (k + 1) * 8, :]
    total = total + pltpu.roll(total, 4, 0)
    root = lax.rsqrt(total * inverse_width + EPSILON)
    root0 = root[3:4, 0:1]
    root1 = root[3:4, HALF : HALF + 1]
    scaled = total * jnp.where(first_ref[...] > 0.5, root0, root1)
    turned = scaled * cos_ref[...] + pltpu.roll(scaled, HALF, 1) * sin_ref[...]
    twice = jnp.concatenate([turned, turned], axis=0).astype(BF16)
    for k in range(n // 16):
        out_ref[k * 16 : (k + 1) * 16, :] = twice


def attend_kernel(scale, rows_ref, limit_ref, cache_ref, out_ref, flat_ref, score_ref):
    flat_ref[...] = rows_ref[...].astype(F32)
    peers = flat_ref.shape[0] // 4
    rows = 2 * peers
    query = jnp.concatenate(
        [flat_ref[pl.ds(i, peers, stride=4), :] for i in range(2)], axis=0
    ).astype(BF16)
    new = flat_ref[pl.ds(2, 16, stride=4), :]
    new_keys = new.astype(BF16)
    new_values = pltpu.roll(new, 8, 0).astype(BF16)
    tokens = cache_ref.shape[0]
    page = HD
    lane8 = iota((8, page), 1)
    chunk = 4 * page

    row = iota((rows, 16), 0)
    col = iota((rows, 16), 1)
    new_ok = (
        (col < 8) & (col % 4 == row % 4) & (col // 4 <= row // peers)
    ) & (limit_ref[0:1, page - 1 : page] > 0)
    new_scores = jnp.where(new_ok, dot_t(query, new_keys) * scale, NEGATIVE)

    best = None
    for start in range(0, tokens, chunk):
        part = dot_t(query, cache_ref[start : start + chunk, 0:HD]) * scale
        for k in range(chunk // page):
            p = start // page + k
            ok = lane8 < limit_ref[:, p : p + 1]
            piece = part[:, k * page : (k + 1) * page].reshape(rows // 8, 8, page)
            piece = jnp.where(ok[None], piece, NEGATIVE).reshape(rows, page)
            score_ref[:, start + k * page : start + (k + 1) * page] = piece
            best = piece if best is None else jnp.maximum(best, piece)
    top = jnp.maximum(
        jnp.max(best, axis=-1, keepdims=True), jnp.max(new_scores, axis=-1, keepdims=True)
    )
    top = jnp.maximum(top, FLOOR)
    new_weights = jnp.exp(new_scores - top)
    total = jnp.sum(new_weights, axis=-1, keepdims=True)
    mixed = dot(new_weights.astype(BF16), new_values)
    sums = jnp.zeros((rows, page), F32)
    for start in range(0, tokens, chunk):
        weights = jnp.exp(score_ref[:, start : start + chunk] - top)
        for k in range(chunk // page):
            sums = sums + weights[:, k * page : (k + 1) * page]
        mixed = mixed + dot(weights.astype(BF16), cache_ref[start : start + chunk, HD : 2 * HD])
    total = total + jnp.sum(sums, axis=-1, keepdims=True)
    stats = jnp.where(iota((rows, HD), 1) < HALF, top, total)
    for i in range(2):
        out_ref[pl.ds(i, peers, stride=4), :] = mixed[i * peers : (i + 1) * peers]
        out_ref[pl.ds(2 + i, peers, stride=4), :] = stats[i * peers : (i + 1) * peers]


def merge_kernel(parts_ref, out_ref):
    peers = parts_ref.shape[0] // 4
    results = []
    for i in range(2):
        mixed = parts_ref[pl.ds(i, peers, stride=4), :]
        stats = parts_ref[pl.ds(2 + i, peers, stride=4), :]
        top = stats[:, 0:1]
        factor = jnp.exp(top - jnp.max(top, axis=0, keepdims=True))
        total = jnp.sum(factor * stats[:, HALF : HALF + 1], axis=0, keepdims=True)
        results.append(jnp.sum(factor * mixed, axis=0, keepdims=True) / total)
    tile = jnp.where(iota((16, HD), 0) % 2 == 0, results[0], results[1]).astype(BF16)
    for k in range(out_ref.shape[0] // 16):
        out_ref[k * 16 : (k + 1) * 16, :] = tile


def output_kernel(rows_ref, w_ref, out_ref):
    rows = rows_ref[...].astype(F32)
    heads = rows.shape[0] // 8
    lhs = jnp.concatenate([rows[h * 8 : (h + 1) * 8] for h in range(heads)], axis=1)
    part = dot(lhs.astype(BF16), w_ref[...])
    for k in range(out_ref.shape[0] // 8):
        out_ref[k * 8 : (k + 1) * 8, :] = part


def deliver_kernel(owners_ref, parts_ref, out_ref):
    total = parts_ref[0:8, :]
    for k in range(1, parts_ref.shape[0] // 8):
        total = total + parts_ref[k * 8 : (k + 1) * 8, :]
    n = out_ref.shape[0]
    row = iota((n, HD), 0)
    slot = row // 4
    result = jnp.zeros((n, HD), F32)
    small = iota((8, HD), 0)
    for b in range(4):
        tile = jnp.zeros((8, HD), F32)
        for ct in range(2):
            for s in range(2):
                piece = total[2 * b + s : 2 * b + s + 1, ct * HD : (ct + 1) * HD]
                tile = jnp.where(small % 4 == 2 * ct + s, piece, tile)
        spread = jnp.concatenate([tile] * (n // 8), axis=0)
        result = jnp.where(slot == owners_ref[b], spread, result)
    out_ref[...] = result.astype(BF16)


def body(hidden, norm_gain, w_query, w_keyval, w_out, cache, page_table, lengths, owners):
    n_steps, n_reqs, width_local = hidden.shape
    peers = lax.axis_size("ctx")
    groups = lax.axis_size("head")
    device_now = lax.axis_index("ctx")
    width_total = width_local * peers
    pages, page_len = cache.shape[0], cache.shape[1]

    def exchange(x, axis):
        return lax.all_to_all(x, axis, 0, 0, tiled=True)

    request = device_now % n_reqs
    head = device_now // n_reqs
    kv_step = head % 2
    steps = jnp.stack([jnp.int32(0), jnp.int32(1), kv_step, jnp.int32(0)])
    steps = jnp.concatenate([steps, steps])
    position = (lengths[request] + steps).astype(F32)
    angles = position[:, None] * frequencies(HD)
    turns = jnp.concatenate([steps[:2] * 0 + 1, jnp.stack([(head < 2).astype(jnp.int32), 0])])
    turns = jnp.concatenate([turns, turns])[:, None] > 0
    cosine = jnp.where(turns, jnp.cos(angles), 1.0)
    sine = jnp.where(turns, jnp.sin(angles), 0.0)
    cosine = jnp.concatenate([cosine, cosine], axis=-1)
    sine = jnp.concatenate([-sine, sine], axis=-1)
    first = jnp.broadcast_to((steps == 0).astype(F32)[:, None], (8, HD))

    global_ids = device_now * pages + jnp.arange(pages, dtype=jnp.int32)
    logical = jnp.arange(page_table.shape[1], dtype=jnp.int32)
    in_page = jnp.clip(lengths[:, None] - logical[None, :] * page_len, 0, page_len)
    limit = jnp.sum(
        jnp.where(page_table[:, :, None] == global_ids[None, None, :], in_page[:, :, None], 0),
        axis=1,
    )
    limit = jnp.pad(
        limit, ((0, 0), (0, HD - 1 - pages))
    )
    flag = jnp.broadcast_to((device_now == 0).astype(jnp.int32), (n_reqs, 1))
    limit = jnp.concatenate([limit, flag], axis=1)
    limit = jnp.concatenate([limit, limit], axis=0)

    with jax.named_scope("project"):
        parts = call(
            project_kernel, jax.ShapeDtypeStruct((4 * peers, HD), F32), n_in=4
        )(hidden, norm_gain.reshape(1, width_local), w_query, w_keyval)
    parts = exchange(parts.reshape(peers, 4, HD), "ctx").reshape(4 * peers, HD)
    with jax.named_scope("finish"):
        rows = call(
            functools.partial(finish_kernel, 1.0 / width_total),
            jax.ShapeDtypeStruct((4 * peers, HD), BF16),
            n_in=4,
        )(parts, cosine, sine, first)
    rows = exchange(rows.reshape(peers, 4, HD), "ctx").reshape(4 * peers, HD)
    tokens = cache.reshape(pages * page_len, 2 * HD)
    with jax.named_scope("attend"):
        parts = call(
            functools.partial(attend_kernel, HD ** (-0.5)),
            jax.ShapeDtypeStruct((4 * peers, HD), F32),
            scratch=[
                pltpu.VMEM((4 * peers, HD), F32),
                pltpu.VMEM((2 * peers, pages * page_len), F32),
            ],
            n_in=3,
        )(rows, limit, tokens)
    parts = exchange(parts.reshape(peers, 4, HD), "ctx").reshape(4 * peers, HD)
    with jax.named_scope("merge"):
        rows = call(merge_kernel, jax.ShapeDtypeStruct((2 * peers, HD), BF16), n_in=1)(parts)
    rows = exchange(rows.reshape(peers, 2, HD), "ctx").reshape(2 * peers, HD)
    with jax.named_scope("output"):
        parts = call(
            output_kernel, jax.ShapeDtypeStruct((8 * groups, width_local), F32), n_in=2
        )(rows, w_out)
    parts = exchange(parts.reshape(groups, 8, width_local), "head")
    with jax.named_scope("deliver"):
        sent = call(
            deliver_kernel, jax.ShapeDtypeStruct((4 * peers, HD), BF16), n_in=2, smem=(0,)
        )(owners, parts.reshape(8 * groups, width_local))
    got = exchange(sent.reshape(peers, 4, HD), "ctx")
    got = got.reshape(peers, width_local // HD, n_steps, HD)
    return jnp.transpose(got, (2, 0, 1, 3)).reshape(1, n_steps, width_total)


def solution(mesh):
    placed = (
        P(None, None, "ctx"),
        P("ctx"),
        P("ctx", "head"),
        P("ctx", "head"),
        P("head", "ctx"),
        P("ctx", None, "head", None),
        P(),
        P(),
        P(),
    )
    return jax.shard_map(
        body, mesh=mesh, in_specs=placed, out_specs=P("ctx", None, None), check_vma=False
    )
```

```python
import functools
import math

import jax
import jax.numpy as jnp
import numpy as np
from jax import lax
from jax.experimental import pallas as pl
from jax.experimental.pallas import tpu as pltpu
from jax.sharding import Mesh, PartitionSpec as P

HD = 128
HALF = HD // 2
EPSILON = 1e-05
NEGATIVE = -1e30
FLOOR = -1e29
F32 = jnp.float32
BF16 = jnp.bfloat16


def frequencies(head_size):
    index = np.arange(head_size // 2)
    inverse = 500000.0 ** (-2.0 * index / head_size)
    wavelength = 2.0 * math.pi / inverse
    smooth = (8192.0 / wavelength - 1.0) / 3.0
    blended = (1.0 - smooth) * inverse / 8.0 + smooth * inverse
    chosen = np.where(
        wavelength < 2048.0, inverse, np.where(wavelength > 8192.0, inverse / 8.0, blended)
    )
    return chosen.astype(np.float32)


def iota(shape, dim):
    return lax.broadcasted_iota(jnp.int32, shape, dim)


def dot(a, b):
    return jnp.dot(a, b, preferred_element_type=F32)


def dot_t(a, b):
    return lax.dot_general(a, b, (((1,), (1,)), ((), ())), preferred_element_type=F32)


def call(kernel, out, spaces, scratch=(), limit=24):
    return pl.pallas_call(
        kernel,
        out_shape=out,
        in_specs=[pl.BlockSpec(memory_space=space) for space in spaces],
        out_specs=pl.BlockSpec(memory_space=pltpu.VMEM),
        scratch_shapes=list(scratch),
        compiler_params=pltpu.CompilerParams(vmem_limit_bytes=limit * 1024 * 1024),
    )


def split2(x):
    high = x.astype(BF16)
    return high, (x - high.astype(F32)).astype(BF16)


def split3(x):
    first = x.astype(BF16).astype(F32)
    rest = x - first
    second = rest.astype(BF16).astype(F32)
    return first, second, rest - second


def project_kernel(
    hidden_hbm, gain_hbm, wq_hbm, wkv_hbm, out_ref, hidden_ref, gain_ref, wq_ref, wkv_ref, sems
):
    chunks = sems.shape[0] - 3
    chunk = wq_ref.shape[1] // chunks
    copies = [
        pltpu.make_async_copy(hidden_hbm, hidden_ref, sems.at[0]),
        pltpu.make_async_copy(gain_hbm, gain_ref, sems.at[1]),
        pltpu.make_async_copy(wkv_hbm, wkv_ref, sems.at[2]),
    ]
    for k in range(chunks):
        cols = pl.ds(k * chunk, chunk)
        copies.append(
            pltpu.make_async_copy(wq_hbm.at[:, cols], wq_ref.at[:, cols], sems.at[3 + k])
        )
    for copy in copies:
        copy.start()
    copies[0].wait()
    copies[1].wait()
    gain = gain_ref[...].astype(F32).reshape(1, gain_ref.shape[0])
    hid = [hidden_ref[s].astype(F32) for s in range(2)]
    width = hid[0].shape[1]
    row = iota((16, width), 0) % 4
    spread = [
        jnp.concatenate([h[b : b + 1] for b in range(4) for _ in range(4)], axis=0) for h in hid
    ]
    scaled = [x * gain for x in spread]
    zero = jnp.zeros_like(scaled[0])
    lhs_q = split2(jnp.where(row == 0, scaled[0], jnp.where(row == 1, scaled[1], zero)))
    lhs_q = jnp.concatenate(lhs_q, axis=0)
    lhs_kv = [split2(jnp.where(row == 2, x, zero)) for x in scaled]
    lhs_kv = jnp.concatenate([p for pair in lhs_kv for p in pair], axis=0)
    squares = [jnp.sum(x * x, axis=-1, keepdims=True) for x in spread]
    square = jnp.where(iota((16, HD), 1) < HALF, squares[0], squares[1])
    square = jnp.where(iota((16, HD), 0) % 4 == 3, square, 0.0)
    copies[2].wait()
    part_kv = dot(lhs_kv, wkv_ref[...])
    part_kv = [part_kv[0:16] + part_kv[16:32], part_kv[32:48] + part_kv[48:64]]
    for k in range(chunks):
        copies[3 + k].wait()
        part_q = dot(lhs_q, wq_ref[:, k * chunk : (k + 1) * chunk])
        part_q = part_q[0:16] + part_q[16:32]
        for g in range(chunk // HD):
            h = k * (chunk // HD) + g
            block = part_q[:, g * HD : (g + 1) * HD] + square
            if h < 4:
                block = block + part_kv[h % 2][:, (h // 2) * HD : (h // 2 + 1) * HD]
            out_ref[h * 16 : (h + 1) * 16, :] = block


def finish_kernel(inverse_width, parts_ref, cos_ref, sin_ref, first_ref, out_ref):
    n = parts_ref.shape[0]
    total = parts_ref[0:8, :]
    for k in range(1, n // 8):
        total = total + parts_ref[k * 8 : (k + 1) * 8, :]
    total = total + pltpu.roll(total, 4, 0)
    root = lax.rsqrt(total * inverse_width + EPSILON)
    root0 = root[3:4, 0:1]
    root1 = root[3:4, HALF : HALF + 1]
    scaled = total * jnp.where(first_ref[...] > 0.5, root0, root1)
    turned = scaled * cos_ref[...] + pltpu.roll(scaled, HALF, 1) * sin_ref[...]
    twice = jnp.concatenate([turned, turned], axis=0).astype(BF16)
    for k in range(n // 16):
        out_ref[k * 16 : (k + 1) * 16, :] = twice


def attend_kernel(scale, rows_ref, limit_ref, keys_ref, values_ref, out_ref, flat_ref, score_ref):
    flat_ref[...] = rows_ref[...].astype(F32)
    peers = flat_ref.shape[0] // 4
    rows = 2 * peers
    query = jnp.concatenate(
        [flat_ref[pl.ds(i, peers, stride=4), :] for i in range(2)], axis=0
    ).astype(BF16)
    new = flat_ref[pl.ds(2, 16, stride=4), :]
    new_keys = new.astype(BF16)
    new_values = pltpu.roll(new, 8, 0).astype(BF16)
    tokens = keys_ref.shape[0]
    page = HD
    lane8 = iota((8, page), 1)
    chunk = 4 * page

    row = iota((rows, 16), 0)
    col = iota((rows, 16), 1)
    new_ok = (
        (col < 8) & (col % 4 == row % 4) & (col // 4 <= row // peers)
    ) & (limit_ref[0:1, page - 1 : page] > 0)
    new_scores = jnp.where(new_ok, dot_t(query, new_keys) * scale, NEGATIVE)

    best = None
    for start in range(0, tokens, chunk):
        part = dot_t(query, keys_ref[start : start + chunk, :]) * scale
        for k in range(chunk // page):
            p = start // page + k
            ok = lane8 < limit_ref[:, p : p + 1]
            piece = part[:, k * page : (k + 1) * page].reshape(rows // 8, 8, page)
            piece = jnp.where(ok[None], piece, NEGATIVE).reshape(rows, page)
            score_ref[:, start + k * page : start + (k + 1) * page] = piece
            best = piece if best is None else jnp.maximum(best, piece)
    top = jnp.maximum(
        jnp.max(best, axis=-1, keepdims=True), jnp.max(new_scores, axis=-1, keepdims=True)
    )
    top = jnp.maximum(top, FLOOR)
    new_weights = jnp.exp(new_scores - top)
    total = jnp.sum(new_weights, axis=-1, keepdims=True)
    mixed = dot(new_weights.astype(BF16), new_values)
    sums = jnp.zeros((rows, page), F32)
    for start in range(0, tokens, chunk):
        weights = jnp.exp(score_ref[:, start : start + chunk] - top)
        for k in range(chunk // page):
            sums = sums + weights[:, k * page : (k + 1) * page]
        pair = jnp.concatenate(split2(weights), axis=0)
        pair = dot(pair, values_ref[start : start + chunk, :])
        mixed = mixed + pair[:rows] + pair[rows:]
    total = total + jnp.sum(sums, axis=-1, keepdims=True)
    post(mixed, top, total, out_ref)


STATS = 16


def post(mixed, top, total, out_ref):
    rows = mixed.shape[0]
    lane = iota((rows, HD), 1)
    stats = jnp.zeros((rows, HD), F32)
    for k, piece in enumerate(split3(top) + split3(total)):
        stats = jnp.where(lane == k, piece, stats)
    stats = jnp.transpose(stats)[0:STATS].astype(BF16)
    mixed = mixed.astype(BF16)
    block = rows + STATS
    for k in range(out_ref.shape[0] // block):
        out_ref[k * block : k * block + rows, :] = mixed
        out_ref[k * block + rows : (k + 1) * block, :] = stats


def merge(parts_ref):
    rows = HD
    block = rows + STATS
    peers = parts_ref.shape[0] // block
    stats = jnp.concatenate(
        [parts_ref[k * block + rows : (k + 1) * block, :].astype(F32) for k in range(peers)],
        axis=0,
    )
    stats = jnp.transpose(stats)
    stats = stats + pltpu.roll(stats, HD - 1, 1) + pltpu.roll(stats, HD - 2, 1)
    leading = iota((rows, HD), 1) % STATS == 0
    top = jnp.max(jnp.where(leading, stats, NEGATIVE), axis=-1, keepdims=True)
    factor = jnp.where(leading, jnp.exp(jnp.where(leading, stats, top) - top), 0.0)
    total = jnp.sum(factor * pltpu.roll(stats, HD - 3, 1), axis=-1, keepdims=True)
    mixed = jnp.zeros((rows, HD), F32)
    for k in range(peers):
        part = parts_ref[k * block : k * block + rows, :].astype(F32)
        mixed = mixed + factor[:, k * STATS : k * STATS + 1] * part
    return mixed, top, total


def merge_kernel(parts_ref, out_ref):
    mixed, top, total = merge(parts_ref)
    post(mixed, top, total, out_ref)


def output_kernel(parts_ref, w_ref, out_ref):
    mixed, _, total = merge(parts_ref)
    rows = mixed / total
    half = rows.shape[0] // 2
    lhs = jnp.concatenate(
        [
            jnp.concatenate([rows[i * half + h * 4 : i * half + h * 4 + 4] for i in range(2)], axis=0)
            for h in range(half // 4)
        ],
        axis=1,
    )
    part = dot(lhs.astype(BF16), w_ref[...])
    for k in range(out_ref.shape[0] // 8):
        out_ref[k * 8 : (k + 1) * 8, :] = part


def deliver_kernel(owners_ref, parts_ref, out_ref):
    total = parts_ref[0:8, :]
    for k in range(1, parts_ref.shape[0] // 8):
        total = total + parts_ref[k * 8 : (k + 1) * 8, :]
    width = total.shape[1]
    out_ref[...] = jnp.zeros_like(out_ref)
    for b in range(4):
        pair = jnp.concatenate([total[b : b + 1], total[4 + b : 5 + b]], axis=0).astype(BF16)
        place = pl.multiple_of(owners_ref[b] * width, width)
        out_ref[:, pl.ds(place, width)] = pair


def body(hidden, norm_gain, w_query, w_keyval, w_out, cache, page_table, lengths, owners):
    n_steps, n_reqs, width_local = hidden.shape
    ctx = ("z", "xc")
    far, near = lax.axis_size("z"), lax.axis_size("xc")
    peers = far * near
    groups = lax.axis_size("head")
    device_now = lax.axis_index(ctx)
    width_total = width_local * peers
    pages, page_len = cache.shape[0], cache.shape[1]
    vmem, hbm, smem = pltpu.VMEM, pl.ANY, pltpu.SMEM

    def exchange(x, axis, dim=0):
        return lax.all_to_all(x, axis, dim, dim, tiled=True)

    with jax.named_scope("project"):
        chunks = 4
        parts = call(
            project_kernel,
            jax.ShapeDtypeStruct((4 * peers, HD), F32),
            [hbm] * 4,
            scratch=[
                pltpu.VMEM(hidden.shape, BF16),
                pltpu.VMEM(norm_gain.shape, BF16),
                pltpu.VMEM(w_query.shape, BF16),
                pltpu.VMEM(w_keyval.shape, BF16),
                pltpu.SemaphoreType.DMA((chunks + 3,)),
            ],
            limit=60,
        )(hidden, norm_gain, w_query, w_keyval)
    parts, lengths, page_table, cache = lax.optimization_barrier(
        (parts, lengths, page_table, cache)
    )
    parts = exchange(parts.reshape(peers, 4, HD), ctx).reshape(4 * peers, HD)

    request = lax.rem(device_now, n_reqs)
    head = lax.div(device_now, n_reqs)
    kv_step = lax.rem(head, 2)
    row = lax.broadcasted_iota(jnp.int32, (8, HD), 0) % 4
    steps = jnp.where(row == 1, 1, jnp.where(row == 2, kv_step, 0))
    turns = (row < 2) | ((row == 2) & (head < 2))
    near_length = lax.dynamic_slice(lengths, (request,), (1,))[0]
    position = (near_length + steps).astype(F32)
    freq = np.concatenate([frequencies(HD)] * 2)
    sign = np.concatenate([-np.ones(HALF, np.float32), np.ones(HALF, np.float32)])
    angles = position * freq[None, :]
    cosine = jnp.where(turns, jnp.cos(angles), 1.0)
    sine = jnp.where(turns, jnp.sin(angles) * sign[None, :], 0.0)
    first = (steps == 0).astype(F32)

    lane = np.arange(HD, dtype=np.int32)
    global_ids = jnp.where(lane < pages, device_now * pages + lane, -2)
    logical = np.arange(page_table.shape[1], dtype=np.int32)
    in_page = jnp.clip(lengths[:, None] - logical[None, :] * page_len, 0, page_len)
    limit = jnp.sum(
        jnp.where(page_table[:, :, None] == global_ids[None, None, :], in_page[:, :, None], 0),
        axis=1,
    )
    limit = limit + jnp.where(lane == HD - 1, (device_now == 0).astype(jnp.int32), 0)[None]
    limit = jnp.concatenate([limit, limit], axis=0)
    tokens = cache.reshape(pages * page_len, 2 * HD)
    keys, values = tokens[:, :HD], tokens[:, HD:]
    parts, cosine, sine, first, limit, keys, values = lax.optimization_barrier(
        (parts, cosine, sine, first, limit, keys, values)
    )

    with jax.named_scope("finish"):
        rows = call(
            functools.partial(finish_kernel, 1.0 / width_total),
            jax.ShapeDtypeStruct((4 * peers, HD), BF16),
            [vmem] * 4,
        )(parts, cosine, sine, first)
    rows = exchange(rows.reshape(peers, 4, HD), ctx).reshape(4 * peers, HD)
    block = 2 * peers + STATS
    with jax.named_scope("attend"):
        parts = call(
            functools.partial(attend_kernel, HD ** (-0.5)),
            jax.ShapeDtypeStruct((near * block, HD), BF16),
            [vmem] * 4,
            scratch=[
                pltpu.VMEM((4 * peers, HD), F32),
                pltpu.VMEM((2 * peers, pages * page_len), F32),
            ],
        )(rows, limit, keys, values)
    parts = exchange(parts.reshape(near, block, HD), "xc").reshape(near * block, HD)
    with jax.named_scope("merge"):
        parts = call(
            merge_kernel, jax.ShapeDtypeStruct((far * block, HD), BF16), [vmem]
        )(parts)
    parts = exchange(parts.reshape(far, block, HD), "z").reshape(far * block, HD)
    with jax.named_scope("output"):
        parts = call(
            output_kernel,
            jax.ShapeDtypeStruct((8 * groups, width_local), F32),
            [vmem] * 2,
        )(parts, w_out)
    parts = exchange(parts.reshape(groups, 8, width_local), "head")
    with jax.named_scope("deliver"):
        sent = call(
            deliver_kernel, jax.ShapeDtypeStruct((n_steps, width_total), BF16), [smem, vmem]
        )(owners, parts.reshape(8 * groups, width_local))
    return exchange(sent, ctx, 1)[None]


def solution(mesh):
    ctx = ("z", "xc")
    near = 8
    split = Mesh(
        mesh.devices.reshape(mesh.shape["ctx"] // near, near, mesh.shape["head"]),
        ("z", "xc", "head"),
    )
    placed = (
        P(None, None, ctx),
        P(ctx),
        P(ctx, "head"),
        P(ctx, "head"),
        P("head", ctx),
        P(ctx, None, "head", None),
        P(),
        P(),
        P(),
    )
    return jax.shard_map(
        body, mesh=split, in_specs=placed, out_specs=P(ctx, None, None), check_vma=False
    )
```

```python
import functools
import math

import jax
import jax.numpy as jnp
import numpy as np
from jax import lax
from jax.experimental import pallas as pl
from jax.experimental.pallas import tpu as pltpu
from jax.sharding import Mesh, PartitionSpec as P

HD = 128
HALF = HD // 2
EPSILON = 1e-05
NEGATIVE = -1e30
FLOOR = -1e29
F32 = jnp.float32
BF16 = jnp.bfloat16


def frequencies(head_size):
    halfway = head_size // 2
    inverse = 500000.0 ** (-(jnp.arange(halfway, dtype=F32) * 2.0 / head_size))
    wavelength = 2.0 * math.pi / inverse
    smooth = (8192.0 / wavelength - 1.0) / 3.0
    blended = (1.0 - smooth) * inverse / 8.0 + smooth * inverse
    return jnp.where(
        wavelength < 2048.0, inverse, jnp.where(wavelength > 8192.0, inverse / 8.0, blended)
    )


def iota(shape, dim):
    return lax.broadcasted_iota(jnp.int32, shape, dim)


def dot(a, b):
    return jnp.dot(a, b, preferred_element_type=F32)


def dot_t(a, b):
    return lax.dot_general(a, b, (((1,), (1,)), ((), ())), preferred_element_type=F32)


def call(kernel, out, spaces, scratch=(), limit=24):
    return pl.pallas_call(
        kernel,
        out_shape=out,
        in_specs=[pl.BlockSpec(memory_space=space) for space in spaces],
        out_specs=pl.BlockSpec(memory_space=pltpu.VMEM),
        scratch_shapes=list(scratch),
        compiler_params=pltpu.CompilerParams(vmem_limit_bytes=limit * 1024 * 1024),
    )


def split2(x):
    high = x.astype(BF16)
    return high, (x - high.astype(F32)).astype(BF16)


def split3(x):
    first = x.astype(BF16).astype(F32)
    rest = x - first
    second = rest.astype(BF16).astype(F32)
    return first, second, rest - second


TILE = 16
CODE = math.log(2.0) / 128.0
TOP = 32000.0


def encode(heads, rest, out_ref):
    scales, marks = [], []
    lane = iota((8, HD), 1)
    largest = jnp.abs(heads[0])
    for x in heads[1:]:
        largest = jnp.maximum(largest, jnp.abs(x))
    mark = jnp.zeros((8, HD), F32)
    for k, x in enumerate([largest] + [jnp.abs(x) for x in rest]):
        most = jnp.maximum(jnp.max(x, axis=-1, keepdims=True), 1e-28)
        exponent = jnp.ceil(jnp.log(most * (1.0 / TOP)) * (1.0 / CODE))
        scales.append(jnp.exp(exponent * -CODE))
        mark = jnp.where(lane // (HD // 4) == k, exponent, mark)
    tiles = [x * scales[0] for x in heads] + [x * s for x, s in zip(rest, scales[1:])] + [mark]
    pairs = [
        jnp.round(jnp.concatenate(tiles[k : k + 2], axis=0)).astype(jnp.int32).astype(jnp.int16)
        for k in range(0, len(tiles), 2)
    ]
    block = TILE * len(pairs)
    for n in range(out_ref.shape[0] // block):
        for k, pair in enumerate(pairs):
            start = n * block + k * TILE
            out_ref[start : start + TILE, :] = pair


def decode(parts_ref, heads):
    pairs = heads // 2 + 2
    block = TILE * pairs
    sums = None
    for n in range(parts_ref.shape[0] // block):
        tiles = [
            parts_ref[n * block + k * TILE : n * block + (k + 1) * TILE, :]
            .astype(jnp.int32)
            .astype(F32)
            for k in range(pairs)
        ]
        scale = jnp.exp(tiles[-1][8:16] * CODE)
        cols = [scale[:, k * (HD // 4) : k * (HD // 4) + 1] for k in range(4)]
        twice = jnp.concatenate([cols[0], cols[0]], axis=0)
        terms = [x * twice for x in tiles[:-2]]
        terms += [tiles[-2][0:8] * cols[1], tiles[-2][8:16] * cols[2], tiles[-1][0:8] * cols[3]]
        sums = terms if sums is None else [x + y for x, y in zip(sums, terms)]
    queries = [x[8 * k : 8 * k + 8] for x in sums[:-3] for k in range(2)]
    return queries, sums[-3:]


def project_kernel(
    hidden_hbm, gain_hbm, wq_hbm, wkv_hbm, out_ref, hidden_ref, gain_ref, wq_ref, wkv_ref, sems
):
    chunks = sems.shape[0] - 3
    chunk = wq_ref.shape[1] // chunks
    copies = [
        pltpu.make_async_copy(hidden_hbm, hidden_ref, sems.at[0]),
        pltpu.make_async_copy(gain_hbm, gain_ref, sems.at[1]),
        pltpu.make_async_copy(wkv_hbm, wkv_ref, sems.at[2]),
    ]
    for k in range(chunks):
        cols = pl.ds(k * chunk, chunk)
        copies.append(
            pltpu.make_async_copy(wq_hbm.at[:, cols], wq_ref.at[:, cols], sems.at[3 + k])
        )
    for copy in copies:
        copy.start()
    copies[0].wait()
    copies[1].wait()
    gain = gain_ref[...].astype(F32).reshape(1, gain_ref.shape[0])
    hid = jnp.concatenate([hidden_ref[s].astype(F32) for s in range(2)], axis=0)
    lhs = jnp.concatenate(split2(hid * gain), axis=0)
    square = jnp.broadcast_to(jnp.sum(hid * hid, axis=-1, keepdims=True), (8, HD))
    copies[2].wait()
    part = dot(lhs, wkv_ref[...])
    part = part[0:8] + part[8:16]
    rest = [part[:, :HD], part[:, HD:], square]
    heads = []
    for k in range(chunks):
        copies[3 + k].wait()
        part = dot(lhs, wq_ref[:, k * chunk : (k + 1) * chunk])
        part = part[0:8] + part[8:16]
        heads += [part[:, g * HD : (g + 1) * HD] for g in range(chunk // HD)]
    encode(heads, rest, out_ref)


def sum_kernel(heads, parts_ref, out_ref):
    encode(*decode(parts_ref, heads), out_ref)


def attend_kernel(
    scale, inverse_width, parts_ref, cos_ref, sin_ref, limit_ref, keys_ref, values_ref, out_ref,
    score_ref,
):
    rows = HD
    queries, (key, value, square) = decode(parts_ref, rows // 8)
    root = lax.rsqrt(square * inverse_width + EPSILON)

    def turn(x):
        x = x * root
        return x * cos_ref[...] + pltpu.roll(x, HALF, 1) * sin_ref[...]

    query = jnp.concatenate([turn(x) for x in queries], axis=0)
    query = jnp.concatenate(split2(query), axis=0)
    new_keys = turn(key)
    new_values = value * root
    new_keys, new_values = [
        jnp.concatenate(pair, axis=0).astype(BF16)
        for pair in ((new_keys, new_values), (new_values, new_keys))
    ]
    tokens = keys_ref.shape[0]
    page = HD
    lane8 = iota((8, page), 1)
    chunk = 4 * page

    def score(keys):
        both = dot_t(query, keys)
        return (both[:rows] + both[rows:]) * scale

    def mix(weights, values):
        both = dot(jnp.concatenate(split2(weights), axis=0), values)
        return both[:rows] + both[rows:]

    row = iota((rows, 16), 0) % 8
    col = iota((rows, 16), 1)
    new_ok = ((col < 8) & (col % 4 == row % 4) & (col // 4 <= row // 4)) & (
        limit_ref[0:1, page - 1 : page] > 0
    )
    new_scores = jnp.where(new_ok, score(new_keys), NEGATIVE)

    best = None
    for start in range(0, tokens, chunk):
        part = score(keys_ref[start : start + chunk, :])
        for k in range(chunk // page):
            p = start // page + k
            ok = lane8 < limit_ref[:, p : p + 1]
            piece = part[:, k * page : (k + 1) * page].reshape(rows // 8, 8, page)
            piece = jnp.where(ok[None], piece, NEGATIVE).reshape(rows, page)
            score_ref[:, start + k * page : start + (k + 1) * page] = piece
            best = piece if best is None else jnp.maximum(best, piece)
    top = jnp.maximum(
        jnp.max(best, axis=-1, keepdims=True), jnp.max(new_scores, axis=-1, keepdims=True)
    )
    top = jnp.maximum(top, FLOOR)
    new_weights = jnp.exp(new_scores - top)
    total = jnp.sum(new_weights, axis=-1, keepdims=True)
    mixed = mix(new_weights, new_values)
    sums = jnp.zeros((rows, page), F32)
    for start in range(0, tokens, chunk):
        weights = jnp.exp(score_ref[:, start : start + chunk] - top)
        for k in range(chunk // page):
            sums = sums + weights[:, k * page : (k + 1) * page]
        mixed = mixed + mix(weights, values_ref[start : start + chunk, :])
    total = total + jnp.sum(sums, axis=-1, keepdims=True)
    post(mixed, top, total, out_ref)


STATS = 16


def post(mixed, top, total, out_ref):
    rows = mixed.shape[0]
    lane = iota((rows, HD), 1)
    stats = jnp.zeros((rows, HD), F32)
    for k, piece in enumerate(split3(top) + split3(total)):
        stats = jnp.where(lane == k, piece, stats)
    stats = jnp.transpose(stats)[0:STATS].astype(BF16)
    mixed = mixed.astype(BF16)
    block = rows + STATS
    for k in range(out_ref.shape[0] // block):
        out_ref[k * block : k * block + rows, :] = mixed
        out_ref[k * block + rows : (k + 1) * block, :] = stats


def merge(parts_ref):
    rows = HD
    block = rows + STATS
    peers = parts_ref.shape[0] // block
    stats = jnp.concatenate(
        [parts_ref[k * block + rows : (k + 1) * block, :].astype(F32) for k in range(peers)],
        axis=0,
    )
    stats = jnp.transpose(stats)
    stats = stats + pltpu.roll(stats, HD - 1, 1) + pltpu.roll(stats, HD - 2, 1)
    leading = iota((rows, HD), 1) % STATS == 0
    top = jnp.max(jnp.where(leading, stats, NEGATIVE), axis=-1, keepdims=True)
    factor = jnp.where(leading, jnp.exp(jnp.where(leading, stats, top) - top), 0.0)
    total = jnp.sum(factor * pltpu.roll(stats, HD - 3, 1), axis=-1, keepdims=True)
    mixed = jnp.zeros((rows, HD), F32)
    for k in range(peers):
        part = parts_ref[k * block : k * block + rows, :].astype(F32)
        mixed = mixed + factor[:, k * STATS : k * STATS + 1] * part
    return mixed, top, total


def merge_kernel(parts_ref, out_ref):
    mixed, top, total = merge(parts_ref)
    post(mixed, top, total, out_ref)


def output_kernel(parts_ref, w_ref, out_ref):
    mixed, _, total = merge(parts_ref)
    rows = mixed / total
    heads = rows.shape[0] // 8
    lhs = jnp.concatenate([rows[h * 8 : h * 8 + 8] for h in range(heads)], axis=1)
    part = dot(jnp.concatenate(split2(lhs), axis=0), w_ref[...])
    part = part[0:8] + part[8:16]
    for k in range(out_ref.shape[0] // 8):
        out_ref[k * 8 : (k + 1) * 8, :] = part


def deliver_kernel(owners_ref, parts_ref, out_ref):
    total = parts_ref[0:8, :]
    for k in range(1, parts_ref.shape[0] // 8):
        total = total + parts_ref[k * 8 : (k + 1) * 8, :]
    width = total.shape[1]
    out_ref[...] = jnp.zeros_like(out_ref)
    for b in range(4):
        pair = jnp.concatenate([total[b : b + 1], total[4 + b : 5 + b]], axis=0).astype(BF16)
        place = pl.multiple_of(owners_ref[b] * width, width)
        out_ref[:, pl.ds(place, width)] = pair


def body(hidden, norm_gain, w_query, w_keyval, w_out, cache, page_table, lengths, owners):
    n_steps, n_reqs, width_local = hidden.shape
    ctx = ("z", "xc")
    far, near = lax.axis_size("z"), lax.axis_size("xc")
    peers = far * near
    groups = lax.axis_size("head")
    device_now = lax.axis_index(ctx)
    width_total = width_local * peers
    pages, page_len = cache.shape[0], cache.shape[1]
    vmem, hbm, smem = pltpu.VMEM, pl.ANY, pltpu.SMEM

    def exchange(x, axis, dim=0):
        return lax.all_to_all(x, axis, dim, dim, tiled=True)

    heads = w_query.shape[1] // HD
    coded = TILE * (heads // 2 + 2)
    block = 8 * heads + STATS

    with jax.named_scope("project"):
        chunks = 4
        parts = call(
            project_kernel,
            jax.ShapeDtypeStruct((near * coded, HD), jnp.int16),
            [hbm] * 4,
            scratch=[
                pltpu.VMEM(hidden.shape, BF16),
                pltpu.VMEM(norm_gain.shape, BF16),
                pltpu.VMEM(w_query.shape, BF16),
                pltpu.VMEM(w_keyval.shape, BF16),
                pltpu.SemaphoreType.DMA((chunks + 3,)),
            ],
            limit=60,
        )(hidden, norm_gain, w_query, w_keyval)
    parts, lengths, page_table, cache = lax.optimization_barrier(
        (parts, lengths, page_table, cache)
    )
    parts = exchange(parts.reshape(near, coded, HD), "xc").reshape(near * coded, HD)

    position = (lengths[None, :] + jnp.arange(n_steps, dtype=jnp.int32)[:, None]).astype(F32)
    angles = position.reshape(n_steps * n_reqs, 1) * frequencies(HD)
    cosine, sine = jnp.cos(angles), jnp.sin(angles)
    cosine = jnp.concatenate([cosine, cosine], axis=-1)
    sine = jnp.concatenate([-sine, sine], axis=-1)

    lane = np.arange(HD, dtype=np.int32)
    global_ids = jnp.where(lane < pages, device_now * pages + lane, -2)
    logical = np.arange(page_table.shape[1], dtype=np.int32)
    in_page = jnp.clip(lengths[:, None] - logical[None, :] * page_len, 0, page_len)
    limit = jnp.sum(
        jnp.where(page_table[:, :, None] == global_ids[None, None, :], in_page[:, :, None], 0),
        axis=1,
    )
    limit = limit + jnp.where(lane == HD - 1, (device_now == 0).astype(jnp.int32), 0)[None]
    limit = jnp.concatenate([limit, limit], axis=0)
    tokens = cache.reshape(pages * page_len, 2 * HD)
    keys, values = tokens[:, :HD], tokens[:, HD:]
    parts, cosine, sine, limit, keys, values = lax.optimization_barrier(
        (parts, cosine, sine, limit, keys, values)
    )

    with jax.named_scope("sum"):
        parts = call(
            functools.partial(sum_kernel, heads),
            jax.ShapeDtypeStruct((far * coded, HD), jnp.int16),
            [vmem],
        )(parts)
    parts = exchange(parts.reshape(far, coded, HD), "z").reshape(far * coded, HD)
    with jax.named_scope("attend"):
        parts = call(
            functools.partial(attend_kernel, HD ** (-0.5), 1.0 / width_total),
            jax.ShapeDtypeStruct((near * block, HD), BF16),
            [vmem] * 6,
            scratch=[pltpu.VMEM((8 * heads, pages * page_len), F32)],
        )(parts, cosine, sine, limit, keys, values)
    parts = exchange(parts.reshape(near, block, HD), "xc").reshape(near * block, HD)
    with jax.named_scope("merge"):
        parts = call(
            merge_kernel, jax.ShapeDtypeStruct((far * block, HD), BF16), [vmem]
        )(parts)
    parts = exchange(parts.reshape(far, block, HD), "z").reshape(far * block, HD)
    with jax.named_scope("output"):
        parts = call(
            output_kernel,
            jax.ShapeDtypeStruct((8 * groups, width_local), F32),
            [vmem] * 2,
        )(parts, w_out)
    parts = exchange(parts.reshape(groups, 8, width_local), "head")
    with jax.named_scope("deliver"):
        sent = call(
            deliver_kernel, jax.ShapeDtypeStruct((n_steps, width_total), BF16), [smem, vmem]
        )(owners, parts.reshape(8 * groups, width_local))
    return exchange(sent, ctx, 1)[None]


def solution(mesh):
    ctx = ("z", "xc")
    near = 8
    split = Mesh(
        mesh.devices.reshape(mesh.shape["ctx"] // near, near, mesh.shape["head"]),
        ("z", "xc", "head"),
    )
    placed = (
        P(None, None, ctx),
        P(ctx),
        P(ctx, "head"),
        P(ctx, "head"),
        P("head", ctx),
        P(ctx, None, "head", None),
        P(),
        P(),
        P(),
    )
    return jax.shard_map(
        body, mesh=split, in_specs=placed, out_specs=P(ctx, None, None), check_vma=False
    )
```

```python
import functools
import math

import jax
import jax.numpy as jnp
import numpy as np
from jax import lax
from jax.experimental import pallas as pl
from jax.experimental.pallas import tpu as pltpu
from jax.sharding import Mesh, PartitionSpec as P

HD = 128
HALF = HD // 2
EPSILON = 1e-05
NEGATIVE = -1e30
FLOOR = -1e29
F32 = jnp.float32
BF16 = jnp.bfloat16


def frequencies(head_size):
    halfway = head_size // 2
    inverse = 500000.0 ** (-(jnp.arange(halfway, dtype=F32) * 2.0 / head_size))
    wavelength = 2.0 * math.pi / inverse
    smooth = (8192.0 / wavelength - 1.0) / 3.0
    blended = (1.0 - smooth) * inverse / 8.0 + smooth * inverse
    return jnp.where(
        wavelength < 2048.0, inverse, jnp.where(wavelength > 8192.0, inverse / 8.0, blended)
    )


def iota(shape, dim):
    return lax.broadcasted_iota(jnp.int32, shape, dim)


def dot(a, b):
    return jnp.dot(a, b, preferred_element_type=F32)


def dot_t(a, b):
    return lax.dot_general(a, b, (((1,), (1,)), ((), ())), preferred_element_type=F32)


def call(kernel, out, spaces, scratch=(), limit=24):
    return pl.pallas_call(
        kernel,
        out_shape=out,
        in_specs=[pl.BlockSpec(memory_space=space) for space in spaces],
        out_specs=pl.BlockSpec(memory_space=pltpu.VMEM),
        scratch_shapes=list(scratch),
        compiler_params=pltpu.CompilerParams(vmem_limit_bytes=limit * 1024 * 1024),
    )


def split2(x):
    high = x.astype(BF16)
    return high, (x - high.astype(F32)).astype(BF16)


def split3(x):
    first = x.astype(BF16).astype(F32)
    rest = x - first
    second = rest.astype(BF16).astype(F32)
    return first, second, rest - second


TILE = 16
CODE = math.log(2.0) / 128.0
TOP = 32000.0


def encode(heads, rest, out_ref):
    scales, marks = [], []
    lane = iota((8, HD), 1)
    largest = jnp.abs(heads[0])
    for x in heads[1:]:
        largest = jnp.maximum(largest, jnp.abs(x))
    mark = jnp.zeros((8, HD), F32)
    for k, x in enumerate([largest] + [jnp.abs(x) for x in rest]):
        most = jnp.maximum(jnp.max(x, axis=-1, keepdims=True), 1e-28)
        exponent = jnp.ceil(jnp.log(most * (1.0 / TOP)) * (1.0 / CODE))
        scales.append(jnp.exp(exponent * -CODE))
        mark = jnp.where(lane // (HD // 4) == k, exponent, mark)
    tiles = [x * scales[0] for x in heads] + [x * s for x, s in zip(rest, scales[1:])] + [mark]
    pairs = [
        jnp.round(jnp.concatenate(tiles[k : k + 2], axis=0)).astype(jnp.int32).astype(jnp.int16)
        for k in range(0, len(tiles), 2)
    ]
    block = TILE * len(pairs)
    for n in range(out_ref.shape[0] // block):
        for k, pair in enumerate(pairs):
            start = n * block + k * TILE
            out_ref[start : start + TILE, :] = pair


def decode(parts_ref, heads):
    pairs = heads // 2 + 2
    block = TILE * pairs
    sums = None
    for n in range(parts_ref.shape[0] // block):
        tiles = [
            parts_ref[n * block + k * TILE : n * block + (k + 1) * TILE, :]
            .astype(jnp.int32)
            .astype(F32)
            for k in range(pairs)
        ]
        scale = jnp.exp(tiles[-1][8:16] * CODE)
        cols = [scale[:, k * (HD // 4) : k * (HD // 4) + 1] for k in range(4)]
        twice = jnp.concatenate([cols[0], cols[0]], axis=0)
        terms = [x * twice for x in tiles[:-2]]
        terms += [tiles[-2][0:8] * cols[1], tiles[-2][8:16] * cols[2], tiles[-1][0:8] * cols[3]]
        sums = terms if sums is None else [x + y for x, y in zip(sums, terms)]
    queries = [x[8 * k : 8 * k + 8] for x in sums[:-3] for k in range(2)]
    return queries, sums[-3:]


def project_kernel(
    hidden_hbm, gain_hbm, wq_hbm, wkv_hbm, out_ref, hidden_ref, gain_ref, wq_ref, wkv_ref, sems
):
    chunks = sems.shape[0] - 3
    chunk = wq_ref.shape[1] // chunks
    copies = [
        pltpu.make_async_copy(hidden_hbm, hidden_ref, sems.at[0]),
        pltpu.make_async_copy(gain_hbm, gain_ref, sems.at[1]),
        pltpu.make_async_copy(wkv_hbm, wkv_ref, sems.at[2]),
    ]
    for k in range(chunks):
        cols = pl.ds(k * chunk, chunk)
        copies.append(
            pltpu.make_async_copy(wq_hbm.at[:, cols], wq_ref.at[:, cols], sems.at[3 + k])
        )
    for copy in copies:
        copy.start()
    copies[0].wait()
    copies[1].wait()
    gain = gain_ref[...].astype(F32).reshape(1, gain_ref.shape[0])
    hid = jnp.concatenate([hidden_ref[s].astype(F32) for s in range(2)], axis=0)
    lhs = jnp.concatenate(split2(hid * gain), axis=0)
    square = jnp.broadcast_to(jnp.sum(hid * hid, axis=-1, keepdims=True), (8, HD))
    copies[2].wait()
    part = dot(lhs, wkv_ref[...])
    part = part[0:8] + part[8:16]
    rest = [part[:, :HD], part[:, HD:], square]
    heads = []
    for k in range(chunks):
        copies[3 + k].wait()
        part = dot(lhs, wq_ref[:, k * chunk : (k + 1) * chunk])
        part = part[0:8] + part[8:16]
        heads += [part[:, g * HD : (g + 1) * HD] for g in range(chunk // HD)]
    encode(heads, rest, out_ref)


def sum_kernel(heads, parts_ref, out_ref):
    encode(*decode(parts_ref, heads), out_ref)


def attend_kernel(
    scale, inverse_width, parts_ref, cos_ref, sin_ref, limit_ref, keys_ref, values_ref, out_ref,
    score_ref,
):
    rows = HD
    queries, (key, value, square) = decode(parts_ref, rows // 8)
    root = lax.rsqrt(square * inverse_width + EPSILON)

    def turn(x):
        x = x * root
        return x * cos_ref[...] + pltpu.roll(x, HALF, 1) * sin_ref[...]

    query = jnp.concatenate([turn(x) for x in queries], axis=0)
    query = jnp.concatenate(split2(query), axis=0)
    new_keys = turn(key)
    new_values = value * root
    new_keys, new_values = [
        jnp.concatenate(pair, axis=0).astype(BF16)
        for pair in ((new_keys, new_values), (new_values, new_keys))
    ]
    tokens = keys_ref.shape[0]
    page = HD
    lane8 = iota((8, page), 1)
    chunk = 4 * page

    def score(keys):
        both = dot_t(query, keys)
        return (both[:rows] + both[rows:]) * scale

    def mix(weights, values):
        both = dot(jnp.concatenate(split2(weights), axis=0), values)
        return both[:rows] + both[rows:]

    row = iota((rows, 16), 0) % 8
    col = iota((rows, 16), 1)
    new_ok = ((col < 8) & (col % 4 == row % 4) & (col // 4 <= row // 4)) & (
        limit_ref[0:1, page - 1 : page] > 0
    )
    new_scores = jnp.where(new_ok, score(new_keys), NEGATIVE)

    best = None
    for start in range(0, tokens, chunk):
        part = score(keys_ref[start : start + chunk, :])
        for k in range(chunk // page):
            p = start // page + k
            ok = lane8 < limit_ref[:, p : p + 1]
            piece = part[:, k * page : (k + 1) * page].reshape(rows // 8, 8, page)
            piece = jnp.where(ok[None], piece, NEGATIVE).reshape(rows, page)
            score_ref[:, start + k * page : start + (k + 1) * page] = piece
            best = piece if best is None else jnp.maximum(best, piece)
    top = jnp.maximum(
        jnp.max(best, axis=-1, keepdims=True), jnp.max(new_scores, axis=-1, keepdims=True)
    )
    top = jnp.maximum(top, FLOOR)
    new_weights = jnp.exp(new_scores - top)
    total = jnp.sum(new_weights, axis=-1, keepdims=True)
    mixed = mix(new_weights, new_values)
    sums = jnp.zeros((rows, page), F32)
    for start in range(0, tokens, chunk):
        weights = jnp.exp(score_ref[:, start : start + chunk] - top)
        for k in range(chunk // page):
            sums = sums + weights[:, k * page : (k + 1) * page]
        mixed = mixed + mix(weights, values_ref[start : start + chunk, :])
    total = total + jnp.sum(sums, axis=-1, keepdims=True)
    post(mixed, tiled(top), tiled(total), out_ref)


STATS = 16
GROUP = 16


def tiled(columns):
    lane = iota((8, HD), 1)
    tile = jnp.zeros((8, HD), F32)
    for h in range(columns.shape[0] // 8):
        tile = jnp.where(lane == h, columns[8 * h : 8 * h + 8], tile)
    return tile


def post(mixed, top, total, out_ref):
    rows = mixed.shape[0]
    tile = jnp.zeros((8, HD), F32)
    for k, piece in enumerate(split3(top) + split3(total)):
        tile = tile + (pltpu.roll(piece, k * GROUP, 1) if k else piece)
    stats = jnp.concatenate([tile, jnp.zeros_like(tile)], axis=0).astype(BF16)
    mixed = mixed.astype(BF16)
    block = rows + STATS
    for k in range(out_ref.shape[0] // block):
        out_ref[k * block : k * block + rows, :] = mixed
        out_ref[k * block + rows : (k + 1) * block, :] = stats


def merge(parts_ref):
    rows = HD
    block = rows + STATS
    peers = parts_ref.shape[0] // block
    tops, totals = [], []
    for k in range(peers):
        tile = parts_ref[k * block + rows : (k + 1) * block, :].astype(F32)[0:8]
        tile = tile + pltpu.roll(tile, HD - GROUP, 1) + pltpu.roll(tile, HD - 2 * GROUP, 1)
        tops.append(tile)
        totals.append(pltpu.roll(tile, HD - 3 * GROUP, 1))
    top = functools.reduce(jnp.maximum, tops)
    factors = [jnp.exp(x - top) for x in tops]
    total = sum(f * t for f, t in zip(factors, totals))
    mixed = []
    for g in range(rows // 16):
        acc = None
        for k in range(peers):
            part = parts_ref[k * block + 16 * g : k * block + 16 * g + 16, :].astype(F32)
            f = factors[k]
            f = jnp.concatenate([f[:, 2 * g : 2 * g + 1], f[:, 2 * g + 1 : 2 * g + 2]], axis=0)
            acc = f * part if acc is None else acc + f * part
        mixed.append(acc)
    return mixed, top, total


def merge_kernel(parts_ref, out_ref):
    mixed, top, total = merge(parts_ref)
    live = iota((8, HD), 1) < GROUP
    post(
        jnp.concatenate(mixed, axis=0), jnp.where(live, top, 0.0), jnp.where(live, total, 0.0), out_ref
    )


def output_kernel(parts_ref, w_ref, out_ref):
    mixed, _, total = merge(parts_ref)
    inverse = 1.0 / jnp.where(iota((8, HD), 1) < GROUP, total, 1.0)
    lhs = jnp.concatenate(
        [
            mixed[h // 2][8 * (h % 2) : 8 * (h % 2) + 8] * inverse[:, h : h + 1]
            for h in range(2 * len(mixed))
        ],
        axis=1,
    )
    part = dot(jnp.concatenate(split2(lhs), axis=0), w_ref[...])
    part = part[0:8] + part[8:16]
    for k in range(out_ref.shape[0] // 8):
        out_ref[k * 8 : (k + 1) * 8, :] = part


def deliver_kernel(owners_ref, parts_ref, out_ref):
    total = parts_ref[0:8, :]
    for k in range(1, parts_ref.shape[0] // 8):
        total = total + parts_ref[k * 8 : (k + 1) * 8, :]
    width = total.shape[1]
    out_ref[...] = jnp.zeros_like(out_ref)
    for b in range(4):
        pair = jnp.concatenate([total[b : b + 1], total[4 + b : 5 + b]], axis=0).astype(BF16)
        place = pl.multiple_of(owners_ref[b] * width, width)
        out_ref[:, pl.ds(place, width)] = pair


def body(hidden, norm_gain, w_query, w_keyval, w_out, cache, page_table, lengths, owners):
    n_steps, n_reqs, width_local = hidden.shape
    ctx = ("z", "xc")
    far, near = lax.axis_size("z"), lax.axis_size("xc")
    peers = far * near
    groups = lax.axis_size("head")
    device_now = lax.axis_index(ctx)
    width_total = width_local * peers
    pages, page_len = cache.shape[0], cache.shape[1]
    vmem, hbm, smem = pltpu.VMEM, pl.ANY, pltpu.SMEM

    def exchange(x, axis, dim=0):
        return lax.all_to_all(x, axis, dim, dim, tiled=True)

    heads = w_query.shape[1] // HD
    coded = TILE * (heads // 2 + 2)
    block = 8 * heads + STATS

    with jax.named_scope("project"):
        chunks = 4
        parts = call(
            project_kernel,
            jax.ShapeDtypeStruct((near * coded, HD), jnp.int16),
            [hbm] * 4,
            scratch=[
                pltpu.VMEM(hidden.shape, BF16),
                pltpu.VMEM(norm_gain.shape, BF16),
                pltpu.VMEM(w_query.shape, BF16),
                pltpu.VMEM(w_keyval.shape, BF16),
                pltpu.SemaphoreType.DMA((chunks + 3,)),
            ],
            limit=60,
        )(hidden, norm_gain, w_query, w_keyval)
    parts, lengths, page_table, cache = lax.optimization_barrier(
        (parts, lengths, page_table, cache)
    )
    parts = exchange(parts.reshape(near, coded, HD), "xc").reshape(near * coded, HD)

    position = (lengths[None, :] + jnp.arange(n_steps, dtype=jnp.int32)[:, None]).astype(F32)
    angles = position.reshape(n_steps * n_reqs, 1) * frequencies(HD)
    cosine, sine = jnp.cos(angles), jnp.sin(angles)
    cosine = jnp.concatenate([cosine, cosine], axis=-1)
    sine = jnp.concatenate([-sine, sine], axis=-1)

    lane = np.arange(HD, dtype=np.int32)
    global_ids = jnp.where(lane < pages, device_now * pages + lane, -2)
    logical = np.arange(page_table.shape[1], dtype=np.int32)
    in_page = jnp.clip(lengths[:, None] - logical[None, :] * page_len, 0, page_len)
    limit = jnp.sum(
        jnp.where(page_table[:, :, None] == global_ids[None, None, :], in_page[:, :, None], 0),
        axis=1,
    )
    limit = limit + jnp.where(lane == HD - 1, (device_now == 0).astype(jnp.int32), 0)[None]
    limit = jnp.concatenate([limit, limit], axis=0)
    tokens = cache.reshape(pages * page_len, 2 * HD)
    keys, values = tokens[:, :HD], tokens[:, HD:]
    parts, cosine, sine, limit, keys, values = lax.optimization_barrier(
        (parts, cosine, sine, limit, keys, values)
    )

    with jax.named_scope("sum"):
        parts = call(
            functools.partial(sum_kernel, heads),
            jax.ShapeDtypeStruct((far * coded, HD), jnp.int16),
            [vmem],
        )(parts)
    parts = exchange(parts.reshape(far, coded, HD), "z").reshape(far * coded, HD)
    with jax.named_scope("attend"):
        parts = call(
            functools.partial(attend_kernel, HD ** (-0.5), 1.0 / width_total),
            jax.ShapeDtypeStruct((near * block, HD), BF16),
            [vmem] * 6,
            scratch=[pltpu.VMEM((8 * heads, pages * page_len), F32)],
        )(parts, cosine, sine, limit, keys, values)
    parts = exchange(parts.reshape(near, block, HD), "xc").reshape(near * block, HD)
    with jax.named_scope("merge"):
        parts = call(
            merge_kernel, jax.ShapeDtypeStruct((far * block, HD), BF16), [vmem]
        )(parts)
    parts = exchange(parts.reshape(far, block, HD), "z").reshape(far * block, HD)
    with jax.named_scope("output"):
        parts = call(
            output_kernel,
            jax.ShapeDtypeStruct((8 * groups, width_local), F32),
            [vmem] * 2,
        )(parts, w_out)
    parts = exchange(parts.reshape(groups, 8, width_local), "head")
    with jax.named_scope("deliver"):
        sent = call(
            deliver_kernel, jax.ShapeDtypeStruct((n_steps, width_total), BF16), [smem, vmem]
        )(owners, parts.reshape(8 * groups, width_local))
    return exchange(sent, ctx, 1)[None]


def solution(mesh):
    ctx = ("z", "xc")
    near = 8
    split = Mesh(
        mesh.devices.reshape(mesh.shape["ctx"] // near, near, mesh.shape["head"]),
        ("z", "xc", "head"),
    )
    placed = (
        P(None, None, ctx),
        P(ctx),
        P(ctx, "head"),
        P(ctx, "head"),
        P("head", ctx),
        P(ctx, None, "head", None),
        P(),
        P(),
        P(),
    )
    return jax.shard_map(
        body, mesh=split, in_specs=placed, out_specs=P(ctx, None, None), check_vma=False
    )
```

```python
import functools
import math

import jax
import jax.numpy as jnp
import numpy as np
from jax import lax
from jax.experimental import pallas as pl
from jax.experimental.pallas import tpu as pltpu
from jax.sharding import Mesh, PartitionSpec as P

HD = 128
HALF = HD // 2
EPSILON = 1e-05
NEGATIVE = -1e30
FLOOR = -1e29
F32 = jnp.float32
BF16 = jnp.bfloat16


def frequencies(head_size):
    halfway = head_size // 2
    inverse = 500000.0 ** (-(jnp.arange(halfway, dtype=F32) * 2.0 / head_size))
    wavelength = 2.0 * math.pi / inverse
    smooth = (8192.0 / wavelength - 1.0) / 3.0
    blended = (1.0 - smooth) * inverse / 8.0 + smooth * inverse
    return jnp.where(
        wavelength < 2048.0, inverse, jnp.where(wavelength > 8192.0, inverse / 8.0, blended)
    )


def iota(shape, dim):
    return lax.broadcasted_iota(jnp.int32, shape, dim)


def dot(a, b):
    return jnp.dot(a, b, preferred_element_type=F32)


def dot_t(a, b):
    return lax.dot_general(a, b, (((1,), (1,)), ((), ())), preferred_element_type=F32)


def call(kernel, out, spaces, scratch=(), limit=24):
    return pl.pallas_call(
        kernel,
        out_shape=out,
        in_specs=[pl.BlockSpec(memory_space=space) for space in spaces],
        out_specs=pl.BlockSpec(memory_space=pltpu.VMEM),
        scratch_shapes=list(scratch),
        compiler_params=pltpu.CompilerParams(vmem_limit_bytes=limit * 1024 * 1024),
    )


def split2(x):
    high = x.astype(BF16)
    return high, (x - high.astype(F32)).astype(BF16)


def split3(x):
    first = x.astype(BF16).astype(F32)
    rest = x - first
    second = rest.astype(BF16).astype(F32)
    return first, second, rest - second


TILE = 16
CODE = math.log(2.0) / 128.0
TOP = 32000.0


def encode(heads, rest, out_ref):
    scales, marks = [], []
    lane = iota((8, HD), 1)
    largest = jnp.abs(heads[0])
    for x in heads[1:]:
        largest = jnp.maximum(largest, jnp.abs(x))
    mark = jnp.zeros((8, HD), F32)
    for k, x in enumerate([largest] + [jnp.abs(x) for x in rest]):
        most = jnp.maximum(jnp.max(x, axis=-1, keepdims=True), 1e-28)
        exponent = jnp.ceil(jnp.log(most * (1.0 / TOP)) * (1.0 / CODE))
        scales.append(jnp.exp(exponent * -CODE))
        mark = jnp.where(lane // (HD // 4) == k, exponent, mark)
    tiles = [x * scales[0] for x in heads] + [x * s for x, s in zip(rest, scales[1:])] + [mark]
    pairs = [
        jnp.round(jnp.concatenate(tiles[k : k + 2], axis=0)).astype(jnp.int32).astype(jnp.int16)
        for k in range(0, len(tiles), 2)
    ]
    block = TILE * len(pairs)
    for n in range(out_ref.shape[0] // block):
        for k, pair in enumerate(pairs):
            start = n * block + k * TILE
            out_ref[start : start + TILE, :] = pair


def decode(parts_ref, heads):
    pairs = heads // 2 + 2
    block = TILE * pairs
    sums = None
    for n in range(parts_ref.shape[0] // block):
        tiles = [
            parts_ref[n * block + k * TILE : n * block + (k + 1) * TILE, :]
            .astype(jnp.int32)
            .astype(F32)
            for k in range(pairs)
        ]
        scale = jnp.exp(tiles[-1][8:16] * CODE)
        cols = [scale[:, k * (HD // 4) : k * (HD // 4) + 1] for k in range(4)]
        twice = jnp.concatenate([cols[0], cols[0]], axis=0)
        terms = [x * twice for x in tiles[:-2]]
        terms += [tiles[-2][0:8] * cols[1], tiles[-2][8:16] * cols[2], tiles[-1][0:8] * cols[3]]
        sums = terms if sums is None else [x + y for x, y in zip(sums, terms)]
    queries = [x[8 * k : 8 * k + 8] for x in sums[:-3] for k in range(2)]
    return queries, sums[-3:]


def project_kernel(
    hidden_hbm, gain_hbm, wq_hbm, wkv_hbm, out_ref, hidden_ref, gain_ref, wq_ref, wkv_ref, sems
):
    chunks = sems.shape[0] - 3
    chunk = wq_ref.shape[1] // chunks
    copies = [
        pltpu.make_async_copy(hidden_hbm, hidden_ref, sems.at[0]),
        pltpu.make_async_copy(gain_hbm, gain_ref, sems.at[1]),
        pltpu.make_async_copy(wkv_hbm, wkv_ref, sems.at[2]),
    ]
    for k in range(chunks):
        cols = pl.ds(k * chunk, chunk)
        copies.append(
            pltpu.make_async_copy(wq_hbm.at[:, cols], wq_ref.at[:, cols], sems.at[3 + k])
        )
    for copy in copies:
        copy.start()
    copies[0].wait()
    copies[1].wait()
    gain = gain_ref[...].astype(F32).reshape(1, gain_ref.shape[0])
    hid = jnp.concatenate([hidden_ref[s].astype(F32) for s in range(2)], axis=0)
    lhs = jnp.concatenate(split2(hid * gain), axis=0)
    square = jnp.broadcast_to(jnp.sum(hid * hid, axis=-1, keepdims=True), (8, HD))
    copies[2].wait()
    part = dot(lhs, wkv_ref[...])
    part = part[0:8] + part[8:16]
    rest = [part[:, :HD], part[:, HD:], square]
    heads = []
    for k in range(chunks):
        copies[3 + k].wait()
        part = dot(lhs, wq_ref[:, k * chunk : (k + 1) * chunk])
        part = part[0:8] + part[8:16]
        heads += [part[:, g * HD : (g + 1) * HD] for g in range(chunk // HD)]
    encode(heads, rest, out_ref)


def half(core_ref, tiles):
    n = len(tiles) // 2
    return [jnp.where(core_ref[0] == 0, a, b) for a, b in zip(tiles[:n], tiles[n:])]


def sum_kernel(heads, core_ref, parts_ref, out_ref):
    queries, rest = decode(parts_ref, heads)
    encode(half(core_ref, queries), rest, out_ref)


def turn_kernel(scale, inverse_width, parts_ref, cos_ref, sin_ref, out_ref):
    queries, (key, value, square) = decode(parts_ref, (out_ref.shape[0] - 16) // 8)
    root = lax.rsqrt(square * inverse_width + EPSILON)

    def turn(x):
        x = x * root
        return x * cos_ref[...] + pltpu.roll(x, HALF, 1) * sin_ref[...]

    rows = [turn(x) * scale for x in queries] + [turn(key), value * root]
    for k, x in enumerate(rows):
        out_ref[8 * k : 8 * k + 8, :] = x


def attend_kernel(rows_ref, limit_ref, keys_ref, values_ref, out_ref, score_ref):
    rows = HD
    span = rows_ref.shape[0] // 2
    query = jnp.concatenate([rows_ref[0 : span - 16, :], rows_ref[span : 2 * span - 16, :]], axis=0)
    query = jnp.concatenate(split2(query), axis=0)
    new_keys = rows_ref[span - 16 : span - 8, :]
    new_values = rows_ref[span - 8 : span, :]
    new_keys, new_values = [
        jnp.concatenate(pair, axis=0).astype(BF16)
        for pair in ((new_keys, new_values), (new_values, new_keys))
    ]
    tokens = keys_ref.shape[0]
    page = HD
    lane8 = iota((8, page), 1)
    chunk = 4 * page

    def score(keys):
        both = dot_t(query, keys)
        return both[:rows] + both[rows:]

    def mix(weights, values):
        both = dot(jnp.concatenate(split2(weights), axis=0), values)
        return both[:rows] + both[rows:]

    row = iota((rows, 16), 0) % 8
    col = iota((rows, 16), 1)
    new_ok = ((col < 8) & (col % 4 == row % 4) & (col // 4 <= row // 4)) & (
        limit_ref[0:1, page - 1 : page] > 0
    )
    new_scores = jnp.where(new_ok, score(new_keys), NEGATIVE)

    best = None
    for start in range(0, tokens, chunk):
        part = score(keys_ref[start : start + chunk, :])
        for k in range(chunk // page):
            p = start // page + k
            ok = lane8 < limit_ref[:, p : p + 1]
            piece = part[:, k * page : (k + 1) * page].reshape(rows // 8, 8, page)
            piece = jnp.where(ok[None], piece, NEGATIVE).reshape(rows, page)
            score_ref[:, start + k * page : start + (k + 1) * page] = piece
            best = piece if best is None else jnp.maximum(best, piece)
    top = jnp.maximum(
        jnp.max(best, axis=-1, keepdims=True), jnp.max(new_scores, axis=-1, keepdims=True)
    )
    top = jnp.maximum(top, FLOOR)
    new_weights = jnp.exp(new_scores - top)
    total = jnp.sum(new_weights, axis=-1, keepdims=True)
    mixed = mix(new_weights, new_values)
    sums = jnp.zeros((rows, page), F32)
    for start in range(0, tokens, chunk):
        weights = jnp.exp(score_ref[:, start : start + chunk] - top)
        for k in range(chunk // page):
            sums = sums + weights[:, k * page : (k + 1) * page]
        mixed = mixed + mix(weights, values_ref[start : start + chunk, :])
    total = total + jnp.sum(sums, axis=-1, keepdims=True)
    post(mixed, tiled(top), tiled(total), out_ref)


STATS = 16
GROUP = 16


def tiled(columns):
    lane = iota((8, HD), 1)
    tile = jnp.zeros((8, HD), F32)
    for h in range(columns.shape[0] // 8):
        tile = jnp.where(lane == h, columns[8 * h : 8 * h + 8], tile)
    return tile


def post(mixed, top, total, out_ref):
    rows = mixed.shape[0]
    tile = jnp.zeros((8, HD), F32)
    for k, piece in enumerate(split3(top) + split3(total)):
        tile = tile + (pltpu.roll(piece, k * GROUP, 1) if k else piece)
    stats = jnp.concatenate([tile, jnp.zeros_like(tile)], axis=0).astype(BF16)
    mixed = mixed.astype(BF16)
    block = rows + STATS
    for k in range(out_ref.shape[0] // block):
        out_ref[k * block : k * block + rows, :] = mixed
        out_ref[k * block + rows : (k + 1) * block, :] = stats


def merge(parts_ref, rows):
    block = rows + STATS
    peers = parts_ref.shape[0] // block
    tops, totals = [], []
    for k in range(peers):
        tile = parts_ref[k * block + rows : (k + 1) * block, :].astype(F32)[0:8]
        tile = tile + pltpu.roll(tile, HD - GROUP, 1) + pltpu.roll(tile, HD - 2 * GROUP, 1)
        tops.append(tile)
        totals.append(pltpu.roll(tile, HD - 3 * GROUP, 1))
    top = functools.reduce(jnp.maximum, tops)
    factors = [jnp.exp(x - top) for x in tops]
    total = sum(f * t for f, t in zip(factors, totals))
    mixed = []
    for g in range(rows // 16):
        acc = None
        for k in range(peers):
            part = parts_ref[k * block + 16 * g : k * block + 16 * g + 16, :].astype(F32)
            f = factors[k]
            f = jnp.concatenate([f[:, 2 * g : 2 * g + 1], f[:, 2 * g + 1 : 2 * g + 2]], axis=0)
            acc = f * part if acc is None else acc + f * part
        mixed.append(acc)
    return mixed, top, total


def merge_kernel(core_ref, parts_ref, out_ref):
    mixed, top, total = merge(parts_ref, HD)
    live = iota((8, HD), 1) < GROUP // 2
    stats = []
    for x in (top, total):
        x = jnp.where(core_ref[0] == 0, x, pltpu.roll(x, HD - GROUP // 2, 1))
        stats.append(jnp.where(live, x, 0.0))
    post(jnp.concatenate(half(core_ref, mixed), axis=0), *stats, out_ref)


def divide_kernel(parts_ref, out_ref):
    heads = out_ref.shape[0] // 8
    mixed, _, total = merge(parts_ref, 8 * heads)
    inverse = 1.0 / jnp.where(iota((8, HD), 1) < heads, total, 1.0)
    for h in range(heads):
        row = mixed[h // 2][8 * (h % 2) : 8 * (h % 2) + 8]
        out_ref[8 * h : 8 * h + 8, :] = row * inverse[:, h : h + 1]


def output_kernel(rows_ref, w_ref, out_ref):
    heads = rows_ref.shape[0] // 8
    lhs = jnp.concatenate([rows_ref[8 * h : 8 * h + 8, :] for h in range(heads)], axis=1)
    part = dot(jnp.concatenate(split2(lhs), axis=0), w_ref[...])
    part = part[0:8] + part[8:16]
    for k in range(out_ref.shape[0] // 8):
        out_ref[k * 8 : (k + 1) * 8, :] = part


def deliver_kernel(owners_ref, parts_ref, out_ref):
    total = parts_ref[0:8, :]
    for k in range(1, parts_ref.shape[0] // 8):
        total = total + parts_ref[k * 8 : (k + 1) * 8, :]
    width = total.shape[1]
    out_ref[...] = jnp.zeros_like(out_ref)
    for b in range(4):
        pair = jnp.concatenate([total[b : b + 1], total[4 + b : 5 + b]], axis=0).astype(BF16)
        place = pl.multiple_of(owners_ref[b] * width, width)
        out_ref[:, pl.ds(place, width)] = pair


def body(hidden, norm_gain, w_query, w_keyval, w_out, cache, page_table, lengths, owners):
    n_steps, n_reqs, width_local = hidden.shape
    ctx, around = ("z", "x", "core"), ("x", "core")
    far, near = lax.axis_size("z"), lax.axis_size(around)
    peers = far * near
    groups = lax.axis_size("head")
    device_now = lax.axis_index(ctx)
    width_total = width_local * peers
    pages, page_len = cache.shape[0], cache.shape[1]
    vmem, hbm, smem = pltpu.VMEM, pl.ANY, pltpu.SMEM

    def exchange(x, axis, dim=0):
        return lax.all_to_all(x, axis, dim, dim, tiled=True)

    heads = w_query.shape[1] // HD
    coded = TILE * (heads // 2 + 2)
    coded_half = TILE * (heads // 4 + 2)
    block, block_half = 8 * heads + STATS, 4 * heads + STATS
    core = lax.axis_index("core").astype(jnp.int32).reshape(1)

    with jax.named_scope("project"):
        chunks = 4
        parts = call(
            project_kernel,
            jax.ShapeDtypeStruct((near * coded, HD), jnp.int16),
            [hbm] * 4,
            scratch=[
                pltpu.VMEM(hidden.shape, BF16),
                pltpu.VMEM(norm_gain.shape, BF16),
                pltpu.VMEM(w_query.shape, BF16),
                pltpu.VMEM(w_keyval.shape, BF16),
                pltpu.SemaphoreType.DMA((chunks + 3,)),
            ],
            limit=60,
        )(hidden, norm_gain, w_query, w_keyval)
    parts, lengths, page_table, cache = lax.optimization_barrier(
        (parts, lengths, page_table, cache)
    )
    parts = exchange(parts.reshape(near, coded, HD), around).reshape(near * coded, HD)

    position = (lengths[None, :] + jnp.arange(n_steps, dtype=jnp.int32)[:, None]).astype(F32)
    angles = position.reshape(n_steps * n_reqs, 1) * frequencies(HD)
    cosine, sine = jnp.cos(angles), jnp.sin(angles)
    cosine = jnp.concatenate([cosine, cosine], axis=-1)
    sine = jnp.concatenate([-sine, sine], axis=-1)

    lane = np.arange(HD, dtype=np.int32)
    global_ids = jnp.where(lane < pages, device_now * pages + lane, -2)
    logical = np.arange(page_table.shape[1], dtype=np.int32)
    in_page = jnp.clip(lengths[:, None] - logical[None, :] * page_len, 0, page_len)
    limit = jnp.sum(
        jnp.where(page_table[:, :, None] == global_ids[None, None, :], in_page[:, :, None], 0),
        axis=1,
    )
    limit = limit + jnp.where(lane == HD - 1, (device_now == 0).astype(jnp.int32), 0)[None]
    limit = jnp.concatenate([limit, limit], axis=0)
    tokens = cache.reshape(pages * page_len, 2 * HD)
    keys, values = tokens[:, :HD], tokens[:, HD:]
    parts, cosine, sine, limit, keys, values = lax.optimization_barrier(
        (parts, cosine, sine, limit, keys, values)
    )

    with jax.named_scope("sum"):
        parts = call(
            functools.partial(sum_kernel, heads),
            jax.ShapeDtypeStruct((far * coded_half, HD), jnp.int16),
            [smem, vmem],
        )(core, parts)
    parts = exchange(parts.reshape(far, coded_half, HD), "z").reshape(far * coded_half, HD)
    with jax.named_scope("turn"):
        rows = call(
            functools.partial(turn_kernel, HD ** (-0.5), 1.0 / width_total),
            jax.ShapeDtypeStruct((4 * heads + 16, HD), F32),
            [vmem] * 3,
        )(parts, cosine, sine)
    rows = lax.all_gather(rows, "core", axis=0, tiled=True)
    with jax.named_scope("attend"):
        parts = call(
            attend_kernel,
            jax.ShapeDtypeStruct((near * block, HD), BF16),
            [vmem] * 4,
            scratch=[pltpu.VMEM((8 * heads, pages * page_len), F32)],
        )(rows, limit, keys, values)
    parts = exchange(parts.reshape(near, block, HD), around).reshape(near * block, HD)
    with jax.named_scope("merge"):
        parts = call(
            merge_kernel, jax.ShapeDtypeStruct((far * block_half, HD), BF16), [smem, vmem]
        )(core, parts)
    parts = exchange(parts.reshape(far, block_half, HD), "z").reshape(far * block_half, HD)
    with jax.named_scope("divide"):
        rows = call(divide_kernel, jax.ShapeDtypeStruct((4 * heads, HD), F32), [vmem])(parts)
    rows = lax.all_gather(rows, "core", axis=0, tiled=True)
    with jax.named_scope("output"):
        parts = call(
            output_kernel,
            jax.ShapeDtypeStruct((8 * groups, width_local), F32),
            [vmem] * 2,
        )(rows, w_out)
    parts = exchange(parts.reshape(groups, 8, width_local), "head")
    with jax.named_scope("deliver"):
        sent = call(
            deliver_kernel, jax.ShapeDtypeStruct((n_steps, width_total), BF16), [smem, vmem]
        )(owners, parts.reshape(8 * groups, width_local))
    return exchange(sent, ctx, 1)[None]


def solution(mesh):
    ctx = ("z", "x", "core")
    x, core = 4, 2
    split = Mesh(
        mesh.devices.reshape(mesh.shape["ctx"] // (x * core), x, core, mesh.shape["head"]),
        ("z", "x", "core", "head"),
    )
    placed = (
        P(None, None, ctx),
        P(ctx),
        P(ctx, "head"),
        P(ctx, "head"),
        P("head", ctx),
        P(ctx, None, "head", None),
        P(),
        P(),
        P(),
    )
    return jax.shard_map(
        body, mesh=split, in_specs=placed, out_specs=P(ctx, None, None), check_vma=False
    )
```

```python
import functools
import math

import jax
import jax.numpy as jnp
import numpy as np
from jax import lax
from jax.experimental import pallas as pl
from jax.experimental.pallas import tpu as pltpu
from jax.sharding import Mesh, PartitionSpec as P

HD = 128
HALF = HD // 2
EPSILON = 1e-05
NEGATIVE = -1e30
FLOOR = -1e29
F32 = jnp.float32
BF16 = jnp.bfloat16


def frequencies(head_size):
    halfway = head_size // 2
    inverse = 500000.0 ** (-(jnp.arange(halfway, dtype=F32) * 2.0 / head_size))
    wavelength = 2.0 * math.pi / inverse
    smooth = (8192.0 / wavelength - 1.0) / 3.0
    blended = (1.0 - smooth) * inverse / 8.0 + smooth * inverse
    return jnp.where(
        wavelength < 2048.0, inverse, jnp.where(wavelength > 8192.0, inverse / 8.0, blended)
    )


def iota(shape, dim):
    return lax.broadcasted_iota(jnp.int32, shape, dim)


def dot(a, b):
    return jnp.dot(a, b, preferred_element_type=F32)


def dot_t(a, b):
    return lax.dot_general(a, b, (((1,), (1,)), ((), ())), preferred_element_type=F32)


def call(kernel, out, spaces, scratch=(), limit=24):
    return pl.pallas_call(
        kernel,
        out_shape=out,
        in_specs=[pl.BlockSpec(memory_space=space) for space in spaces],
        out_specs=pl.BlockSpec(memory_space=pltpu.VMEM),
        scratch_shapes=list(scratch),
        compiler_params=pltpu.CompilerParams(vmem_limit_bytes=limit * 1024 * 1024),
    )


def split2(x):
    high = x.astype(BF16)
    return high, (x - high.astype(F32)).astype(BF16)


def split3(x):
    first = x.astype(BF16).astype(F32)
    rest = x - first
    second = rest.astype(BF16).astype(F32)
    return first, second, rest - second


TILE = 16
CODE = math.log(2.0) / 128.0
TOP = 32000.0


def encode(heads, rest, out_ref):
    scales, marks = [], []
    lane = iota((8, HD), 1)
    largest = jnp.abs(heads[0])
    for x in heads[1:]:
        largest = jnp.maximum(largest, jnp.abs(x))
    mark = jnp.zeros((8, HD), F32)
    for k, x in enumerate([largest] + [jnp.abs(x) for x in rest]):
        most = jnp.maximum(jnp.max(x, axis=-1, keepdims=True), 1e-28)
        exponent = jnp.ceil(jnp.log(most * (1.0 / TOP)) * (1.0 / CODE))
        scales.append(jnp.exp(exponent * -CODE))
        mark = jnp.where(lane // (HD // 4) == k, exponent, mark)
    tiles = [x * scales[0] for x in heads] + [x * s for x, s in zip(rest, scales[1:])] + [mark]
    pairs = [
        jnp.round(jnp.concatenate(tiles[k : k + 2], axis=0)).astype(jnp.int32).astype(jnp.int16)
        for k in range(0, len(tiles), 2)
    ]
    block = TILE * len(pairs)
    for n in range(out_ref.shape[0] // block):
        for k, pair in enumerate(pairs):
            start = n * block + k * TILE
            out_ref[start : start + TILE, :] = pair


def decode(parts_ref, heads, first=0, step=1):
    pairs = heads // 2 + 2
    block = TILE * pairs
    sums = None
    for n in range(first, parts_ref.shape[0] // block, step):
        tiles = [
            parts_ref[n * block + k * TILE : n * block + (k + 1) * TILE, :]
            .astype(jnp.int32)
            .astype(F32)
            for k in range(pairs)
        ]
        scale = jnp.exp(tiles[-1][8:16] * CODE)
        cols = [scale[:, k * (HD // 4) : k * (HD // 4) + 1] for k in range(4)]
        twice = jnp.concatenate([cols[0], cols[0]], axis=0)
        terms = [x * twice for x in tiles[:-2]]
        terms += [tiles[-2][0:8] * cols[1], tiles[-2][8:16] * cols[2], tiles[-1][0:8] * cols[3]]
        sums = terms if sums is None else [x + y for x, y in zip(sums, terms)]
    queries = [x[8 * k : 8 * k + 8] for x in sums[:-3] for k in range(2)]
    return queries, sums[-3:]


def project_kernel(
    hidden_hbm, gain_hbm, wq_hbm, wkv_hbm, out_ref, hidden_ref, gain_ref, wq_ref, wkv_ref, sems
):
    chunks = sems.shape[0] - 3
    chunk = wq_ref.shape[1] // chunks
    copies = [
        pltpu.make_async_copy(hidden_hbm, hidden_ref, sems.at[0]),
        pltpu.make_async_copy(gain_hbm, gain_ref, sems.at[1]),
        pltpu.make_async_copy(wkv_hbm, wkv_ref, sems.at[2]),
    ]
    for k in range(chunks):
        cols = pl.ds(k * chunk, chunk)
        copies.append(
            pltpu.make_async_copy(wq_hbm.at[:, cols], wq_ref.at[:, cols], sems.at[3 + k])
        )
    for copy in copies:
        copy.start()
    copies[0].wait()
    copies[1].wait()
    gain = gain_ref[...].astype(F32).reshape(1, gain_ref.shape[0])
    hid = jnp.concatenate([hidden_ref[s].astype(F32) for s in range(2)], axis=0)
    lhs = jnp.concatenate(split2(hid * gain), axis=0)
    square = jnp.broadcast_to(jnp.sum(hid * hid, axis=-1, keepdims=True), (8, HD))
    copies[2].wait()
    part = dot(lhs, wkv_ref[...])
    part = part[0:8] + part[8:16]
    rest = [part[:, :HD], part[:, HD:], square]
    heads = []
    for k in range(chunks):
        copies[3 + k].wait()
        part = dot(lhs, wq_ref[:, k * chunk : (k + 1) * chunk])
        part = part[0:8] + part[8:16]
        heads += [part[:, g * HD : (g + 1) * HD] for g in range(chunk // HD)]
    for k, x in enumerate(heads + rest):
        out_ref[8 * k : 8 * k + 8, :] = x


def half(core_ref, tiles):
    n = len(tiles) // 2
    return [jnp.where(core_ref[0] == 0, a, b) for a, b in zip(tiles[:n], tiles[n:])]


def pair_kernel(core_ref, rows_ref, out_ref):
    n = rows_ref.shape[0] // 2
    tiles = [rows_ref[k : k + 8, :] + rows_ref[n + k : n + k + 8, :] for k in range(0, n, 8)]
    encode(half(core_ref, tiles[:-3]), tiles[-3:], out_ref)


def sum_kernel(heads, parts_ref, out_ref):
    encode(*decode(parts_ref, heads), out_ref)


def attend_kernel(
    scale, inverse_width, parts_ref, cos_ref, sin_ref, limit_ref, keys_ref, values_ref, out_ref,
    score_ref,
):
    rows = HD
    queries, (key, value, square) = decode(parts_ref, rows // 16, 0, 2)
    queries += decode(parts_ref, rows // 16, 1, 2)[0]
    root = lax.rsqrt(square * inverse_width + EPSILON)

    def turn(x):
        x = x * root
        return x * cos_ref[...] + pltpu.roll(x, HALF, 1) * sin_ref[...]

    query = jnp.concatenate([turn(x) * scale for x in queries], axis=0)
    query = jnp.concatenate(split2(query), axis=0)
    new_keys, new_values = turn(key), value * root
    new_keys, new_values = [
        jnp.concatenate(pair, axis=0).astype(BF16)
        for pair in ((new_keys, new_values), (new_values, new_keys))
    ]
    tokens = keys_ref.shape[0]
    page = HD
    lane8 = iota((8, page), 1)
    chunk = 4 * page

    def score(keys):
        both = dot_t(query, keys)
        return both[:rows] + both[rows:]

    def mix(weights, values):
        both = dot(jnp.concatenate(split2(weights), axis=0), values)
        return both[:rows] + both[rows:]

    row = iota((rows, 16), 0) % 8
    col = iota((rows, 16), 1)
    new_ok = ((col < 8) & (col % 4 == row % 4) & (col // 4 <= row // 4)) & (
        limit_ref[0:1, page - 1 : page] > 0
    )
    new_scores = jnp.where(new_ok, score(new_keys), NEGATIVE)

    best = None
    for start in range(0, tokens, chunk):
        part = score(keys_ref[start : start + chunk, :])
        for k in range(chunk // page):
            p = start // page + k
            ok = lane8 < limit_ref[:, p : p + 1]
            piece = part[:, k * page : (k + 1) * page].reshape(rows // 8, 8, page)
            piece = jnp.where(ok[None], piece, NEGATIVE).reshape(rows, page)
            score_ref[:, start + k * page : start + (k + 1) * page] = piece
            best = piece if best is None else jnp.maximum(best, piece)
    top = jnp.maximum(
        jnp.max(best, axis=-1, keepdims=True), jnp.max(new_scores, axis=-1, keepdims=True)
    )
    top = jnp.maximum(top, FLOOR)
    new_weights = jnp.exp(new_scores - top)
    total = jnp.sum(new_weights, axis=-1, keepdims=True)
    mixed = mix(new_weights, new_values)
    sums = jnp.zeros((rows, page), F32)
    for start in range(0, tokens, chunk):
        weights = jnp.exp(score_ref[:, start : start + chunk] - top)
        for k in range(chunk // page):
            sums = sums + weights[:, k * page : (k + 1) * page]
        mixed = mixed + mix(weights, values_ref[start : start + chunk, :])
    total = total + jnp.sum(sums, axis=-1, keepdims=True)
    out_ref[0:rows, :] = mixed
    out_ref[rows : rows + 8, :] = tiled(top) + pltpu.roll(tiled(total), GROUP, 1)


STATS = 16
GROUP = 16


def tiled(columns):
    lane = iota((8, HD), 1)
    tile = jnp.zeros((8, HD), F32)
    for h in range(columns.shape[0] // 8):
        tile = jnp.where(lane == h, columns[8 * h : 8 * h + 8], tile)
    return tile


def post(mixed, top, total, out_ref):
    rows = mixed.shape[0]
    tile = jnp.zeros((8, HD), F32)
    for k, piece in enumerate(split3(top) + split3(total)):
        tile = tile + (pltpu.roll(piece, k * GROUP, 1) if k else piece)
    stats = jnp.concatenate([tile, jnp.zeros_like(tile)], axis=0).astype(BF16)
    mixed = mixed.astype(BF16)
    block = rows + STATS
    for k in range(out_ref.shape[0] // block):
        out_ref[k * block : k * block + rows, :] = mixed
        out_ref[k * block + rows : (k + 1) * block, :] = stats


def merge(parts_ref, rows, first=0, step=1):
    block = rows + STATS
    peers = range(first, parts_ref.shape[0] // block, step)
    tops, totals = [], []
    for k in peers:
        tile = parts_ref[k * block + rows : (k + 1) * block, :].astype(F32)[0:8]
        tile = tile + pltpu.roll(tile, HD - GROUP, 1) + pltpu.roll(tile, HD - 2 * GROUP, 1)
        tops.append(tile)
        totals.append(pltpu.roll(tile, HD - 3 * GROUP, 1))
    top = functools.reduce(jnp.maximum, tops)
    factors = [jnp.exp(x - top) for x in tops]
    total = sum(f * t for f, t in zip(factors, totals))
    mixed = []
    for g in range(rows // 16):
        acc = None
        for k, f in zip(peers, factors):
            part = parts_ref[k * block + 16 * g : k * block + 16 * g + 16, :].astype(F32)
            f = jnp.concatenate([f[:, 2 * g : 2 * g + 1], f[:, 2 * g + 1 : 2 * g + 2]], axis=0)
            acc = f * part if acc is None else acc + f * part
        mixed.append(acc)
    return mixed, top, total


def join_kernel(core_ref, rows_ref, out_ref):
    n = rows_ref.shape[0] // 2
    tops = [rows_ref[k * n + n - 8 : k * n + n, :] for k in range(2)]
    totals = [pltpu.roll(x, HD - GROUP, 1) for x in tops]
    top = jnp.maximum(tops[0], tops[1])
    factors = [jnp.exp(x - top) for x in tops]
    total = factors[0] * totals[0] + factors[1] * totals[1]
    mixed = [
        sum(
            factors[k][:, h : h + 1] * rows_ref[k * n + 8 * h : k * n + 8 * h + 8, :]
            for k in range(2)
        )
        for h in range(n // 8 - 1)
    ]
    live = iota((8, HD), 1) < GROUP // 2
    stats = []
    for x in (top, total):
        x = jnp.where(core_ref[0] == 0, x, pltpu.roll(x, HD - GROUP // 2, 1))
        stats.append(jnp.where(live, x, 0.0))
    post(jnp.concatenate(half(core_ref, mixed), axis=0), *stats, out_ref)


def merge_kernel(heads, parts_ref, out_ref):
    mixed, top, total = merge(parts_ref, 8 * heads)
    live = iota((8, HD), 1) < heads
    stats = [jnp.where(live, x, 0.0) for x in (top, total)]
    post(jnp.concatenate(mixed, axis=0), *stats, out_ref)


def output_kernel(heads, parts_ref, w_ref, out_ref):
    lhs = []
    for core in range(2):
        mixed, _, total = merge(parts_ref, 8 * heads, core, 2)
        inverse = 1.0 / jnp.where(iota((8, HD), 1) < heads, total, 1.0)
        for h in range(heads):
            row = mixed[h // 2][8 * (h % 2) : 8 * (h % 2) + 8]
            lhs.append(row * inverse[:, h : h + 1])
    lhs = jnp.concatenate(lhs, axis=1)
    part = dot(jnp.concatenate(split2(lhs), axis=0), w_ref[...])
    part = part[0:8] + part[8:16]
    for k in range(out_ref.shape[0] // 8):
        out_ref[k * 8 : (k + 1) * 8, :] = part


def deliver_kernel(owners_ref, parts_ref, out_ref):
    total = parts_ref[0:8, :]
    for k in range(1, parts_ref.shape[0] // 8):
        total = total + parts_ref[k * 8 : (k + 1) * 8, :]
    width = total.shape[1]
    out_ref[...] = jnp.zeros_like(out_ref)
    for b in range(4):
        pair = jnp.concatenate([total[b : b + 1], total[4 + b : 5 + b]], axis=0).astype(BF16)
        place = pl.multiple_of(owners_ref[b] * width, width)
        out_ref[:, pl.ds(place, width)] = pair


def body(hidden, norm_gain, w_query, w_keyval, w_out, cache, page_table, lengths, owners):
    n_steps, n_reqs, width_local = hidden.shape
    ctx, around = ("z", "x", "core"), ("x", "core")
    far, near = lax.axis_size("z"), lax.axis_size(around)
    peers = far * near
    groups = lax.axis_size("head")
    device_now = lax.axis_index(ctx)
    width_total = width_local * peers
    pages, page_len = cache.shape[0], cache.shape[1]
    vmem, hbm, smem = pltpu.VMEM, pl.ANY, pltpu.SMEM

    def exchange(x, axis, dim=0):
        return lax.all_to_all(x, axis, dim, dim, tiled=True)

    heads = w_query.shape[1] // HD
    coded, block = TILE * (heads // 4 + 2), 4 * heads + STATS
    core = lax.axis_index("core").astype(jnp.int32).reshape(1)

    with jax.named_scope("project"):
        chunks = 4
        parts = call(
            project_kernel,
            jax.ShapeDtypeStruct((8 * (heads + 3), HD), F32),
            [hbm] * 4,
            scratch=[
                pltpu.VMEM(hidden.shape, BF16),
                pltpu.VMEM(norm_gain.shape, BF16),
                pltpu.VMEM(w_query.shape, BF16),
                pltpu.VMEM(w_keyval.shape, BF16),
                pltpu.SemaphoreType.DMA((chunks + 3,)),
            ],
            limit=60,
        )(hidden, norm_gain, w_query, w_keyval)
    parts = lax.all_gather(parts, "core", axis=0, tiled=True)
    with jax.named_scope("pair"):
        parts = call(
            pair_kernel, jax.ShapeDtypeStruct((far * coded, HD), jnp.int16), [smem, vmem]
        )(core, parts)
    parts, lengths, page_table, cache = lax.optimization_barrier(
        (parts, lengths, page_table, cache)
    )
    parts = exchange(parts.reshape(far, coded, HD), "z").reshape(far * coded, HD)

    position = (lengths[None, :] + jnp.arange(n_steps, dtype=jnp.int32)[:, None]).astype(F32)
    angles = position.reshape(n_steps * n_reqs, 1) * frequencies(HD)
    cosine, sine = jnp.cos(angles), jnp.sin(angles)
    cosine = jnp.concatenate([cosine, cosine], axis=-1)
    sine = jnp.concatenate([-sine, sine], axis=-1)

    lane = np.arange(HD, dtype=np.int32)
    global_ids = jnp.where(lane < pages, device_now * pages + lane, -2)
    logical = np.arange(page_table.shape[1], dtype=np.int32)
    in_page = jnp.clip(lengths[:, None] - logical[None, :] * page_len, 0, page_len)
    limit = jnp.sum(
        jnp.where(page_table[:, :, None] == global_ids[None, None, :], in_page[:, :, None], 0),
        axis=1,
    )
    limit = limit + jnp.where(lane == HD - 1, (device_now == 0).astype(jnp.int32), 0)[None]
    limit = jnp.concatenate([limit, limit], axis=0)
    tokens = cache.reshape(pages * page_len, 2 * HD)
    keys, values = tokens[:, :HD], tokens[:, HD:]
    parts, cosine, sine, limit, keys, values = lax.optimization_barrier(
        (parts, cosine, sine, limit, keys, values)
    )

    with jax.named_scope("sum"):
        parts = call(
            functools.partial(sum_kernel, heads // 2),
            jax.ShapeDtypeStruct((near * coded, HD), jnp.int16),
            [vmem],
        )(parts)
    parts = exchange(parts.reshape(near, coded, HD), around).reshape(near * coded, HD)
    with jax.named_scope("attend"):
        parts = call(
            functools.partial(attend_kernel, HD ** (-0.5), 1.0 / width_total),
            jax.ShapeDtypeStruct((8 * heads + 8, HD), F32),
            [vmem] * 6,
            scratch=[pltpu.VMEM((8 * heads, pages * page_len), F32)],
        )(parts, cosine, sine, limit, keys, values)
    parts = lax.all_gather(parts, "core", axis=0, tiled=True)
    with jax.named_scope("join"):
        parts = call(
            join_kernel, jax.ShapeDtypeStruct((far * block, HD), BF16), [smem, vmem]
        )(core, parts)
    parts = exchange(parts.reshape(far, block, HD), "z").reshape(far * block, HD)
    with jax.named_scope("merge"):
        parts = call(
            functools.partial(merge_kernel, heads // 2),
            jax.ShapeDtypeStruct((near * block, HD), BF16),
            [vmem],
        )(parts)
    parts = exchange(parts.reshape(near, block, HD), around).reshape(near * block, HD)
    with jax.named_scope("output"):
        parts = call(
            functools.partial(output_kernel, heads // 2),
            jax.ShapeDtypeStruct((8 * groups, width_local), F32),
            [vmem] * 2,
        )(parts, w_out)
    parts = exchange(parts.reshape(groups, 8, width_local), "head")
    with jax.named_scope("deliver"):
        sent = call(
            deliver_kernel, jax.ShapeDtypeStruct((n_steps, width_total), BF16), [smem, vmem]
        )(owners, parts.reshape(8 * groups, width_local))
    return exchange(sent, ctx, 1)[None]


def solution(mesh):
    ctx = ("z", "x", "core")
    x, core = 4, 2
    split = Mesh(
        mesh.devices.reshape(mesh.shape["ctx"] // (x * core), x, core, mesh.shape["head"]),
        ("z", "x", "core", "head"),
    )
    placed = (
        P(None, None, ctx),
        P(ctx),
        P(ctx, "head"),
        P(ctx, "head"),
        P("head", ctx),
        P(ctx, None, "head", None),
        P(),
        P(),
        P(),
    )
    return jax.shard_map(
        body, mesh=split, in_specs=placed, out_specs=P(ctx, None, None), check_vma=False
    )
```

```python
import functools
import math

import jax
import jax.numpy as jnp
import numpy as np
from jax import lax
from jax.experimental import pallas as pl
from jax.experimental.pallas import tpu as pltpu
from jax.sharding import Mesh, PartitionSpec as P

HD = 128
HALF = HD // 2
EPSILON = 1e-05
NEGATIVE = -1e30
FLOOR = -1e29
F32 = jnp.float32
BF16 = jnp.bfloat16


def frequencies(head_size):
    halfway = head_size // 2
    inverse = 500000.0 ** (-(jnp.arange(halfway, dtype=F32) * 2.0 / head_size))
    wavelength = 2.0 * math.pi / inverse
    smooth = (8192.0 / wavelength - 1.0) / 3.0
    blended = (1.0 - smooth) * inverse / 8.0 + smooth * inverse
    return jnp.where(
        wavelength < 2048.0, inverse, jnp.where(wavelength > 8192.0, inverse / 8.0, blended)
    )


def iota(shape, dim):
    return lax.broadcasted_iota(jnp.int32, shape, dim)


def dot(a, b):
    return jnp.dot(a, b, preferred_element_type=F32)


def dot_t(a, b):
    return lax.dot_general(a, b, (((1,), (1,)), ((), ())), preferred_element_type=F32)


def call(kernel, out, spaces, scratch=(), limit=24):
    return pl.pallas_call(
        kernel,
        out_shape=out,
        in_specs=[pl.BlockSpec(memory_space=space) for space in spaces],
        out_specs=pl.BlockSpec(memory_space=pltpu.VMEM),
        scratch_shapes=list(scratch),
        compiler_params=pltpu.CompilerParams(vmem_limit_bytes=limit * 1024 * 1024),
    )


def split2(x):
    high = x.astype(BF16)
    return high, (x - high.astype(F32)).astype(BF16)


def split3(x):
    first = x.astype(BF16).astype(F32)
    rest = x - first
    second = rest.astype(BF16).astype(F32)
    return first, second, rest - second


TILE = 16
CODE = math.log(2.0) / 128.0
TOP = 32000.0


def encode(heads, rest, out_ref):
    scales, marks = [], []
    lane = iota((8, HD), 1)
    largest = jnp.abs(heads[0])
    for x in heads[1:]:
        largest = jnp.maximum(largest, jnp.abs(x))
    mark = jnp.zeros((8, HD), F32)
    for k, x in enumerate([largest] + [jnp.abs(x) for x in rest]):
        most = jnp.maximum(jnp.max(x, axis=-1, keepdims=True), 1e-28)
        exponent = jnp.ceil(jnp.log(most * (1.0 / TOP)) * (1.0 / CODE))
        scales.append(jnp.exp(exponent * -CODE))
        mark = jnp.where(lane // (HD // 4) == k, exponent, mark)
    tiles = [x * scales[0] for x in heads] + [x * s for x, s in zip(rest, scales[1:])] + [mark]
    pairs = [
        jnp.round(jnp.concatenate(tiles[k : k + 2], axis=0)).astype(jnp.int32).astype(jnp.int16)
        for k in range(0, len(tiles), 2)
    ]
    block = TILE * len(pairs)
    for n in range(out_ref.shape[0] // block):
        for k, pair in enumerate(pairs):
            start = n * block + k * TILE
            out_ref[start : start + TILE, :] = pair


def decode(parts_ref, heads, first=0, step=1):
    pairs = heads // 2 + 2
    block = TILE * pairs
    sums = None
    for n in range(first, parts_ref.shape[0] // block, step):
        tiles = [
            parts_ref[n * block + k * TILE : n * block + (k + 1) * TILE, :]
            .astype(jnp.int32)
            .astype(F32)
            for k in range(pairs)
        ]
        scale = jnp.exp(tiles[-1][8:16] * CODE)
        cols = [scale[:, k * (HD // 4) : k * (HD // 4) + 1] for k in range(4)]
        twice = jnp.concatenate([cols[0], cols[0]], axis=0)
        terms = [x * twice for x in tiles[:-2]]
        terms += [tiles[-2][0:8] * cols[1], tiles[-2][8:16] * cols[2], tiles[-1][0:8] * cols[3]]
        sums = terms if sums is None else [x + y for x, y in zip(sums, terms)]
    queries = [x[8 * k : 8 * k + 8] for x in sums[:-3] for k in range(2)]
    return queries, sums[-3:]


def project_kernel(
    hidden_hbm, gain_hbm, wq_hbm, wkv_hbm, out_ref, hidden_ref, gain_ref, wq_ref, wkv_ref, sems
):
    chunks = sems.shape[0] - 3
    chunk = wq_ref.shape[1] // chunks
    copies = [
        pltpu.make_async_copy(hidden_hbm, hidden_ref, sems.at[0]),
        pltpu.make_async_copy(gain_hbm, gain_ref, sems.at[1]),
        pltpu.make_async_copy(wkv_hbm, wkv_ref, sems.at[2]),
    ]
    for k in range(chunks):
        cols = pl.ds(k * chunk, chunk)
        copies.append(
            pltpu.make_async_copy(wq_hbm.at[:, cols], wq_ref.at[:, cols], sems.at[3 + k])
        )
    for copy in copies:
        copy.start()
    copies[0].wait()
    copies[1].wait()
    gain = gain_ref[...].astype(F32).reshape(1, gain_ref.shape[0])
    hid = jnp.concatenate([hidden_ref[s].astype(F32) for s in range(2)], axis=0)
    lhs = jnp.concatenate(split2(hid * gain), axis=0)
    square = jnp.broadcast_to(jnp.sum(hid * hid, axis=-1, keepdims=True), (8, HD))
    copies[2].wait()
    part = dot(lhs, wkv_ref[...])
    part = part[0:8] + part[8:16]
    rest = [part[:, :HD], part[:, HD:], square]
    heads = []
    for k in range(chunks):
        copies[3 + k].wait()
        part = dot(lhs, wq_ref[:, k * chunk : (k + 1) * chunk])
        part = part[0:8] + part[8:16]
        heads += [part[:, g * HD : (g + 1) * HD] for g in range(chunk // HD)]
    for k, x in enumerate(heads + rest):
        out_ref[8 * k : 8 * k + 8, :] = x


def half(core_ref, tiles):
    n = len(tiles) // 2
    return [jnp.where(core_ref[0] == 0, a, b) for a, b in zip(tiles[:n], tiles[n:])]


def pair_kernel(core_ref, rows_ref, out_ref):
    n = rows_ref.shape[0] // 2
    tiles = [rows_ref[k : k + 8, :] + rows_ref[n + k : n + k + 8, :] for k in range(0, n, 8)]
    encode(half(core_ref, tiles[:-3]), tiles[-3:], out_ref)


def sum_kernel(heads, parts_ref, out_ref):
    encode(*decode(parts_ref, heads), out_ref)


def attend_kernel(
    scale, inverse_width, parts_ref, cos_ref, sin_ref, limit_ref, keys_ref, values_ref, out_ref,
    score_ref,
):
    rows = HD
    queries, (key, value, square) = decode(parts_ref, rows // 16, 0, 2)
    queries += decode(parts_ref, rows // 16, 1, 2)[0]
    root = lax.rsqrt(square * inverse_width + EPSILON)

    def turn(x):
        x = x * root
        return x * cos_ref[...] + pltpu.roll(x, HALF, 1) * sin_ref[...]

    query = jnp.concatenate([turn(x) * scale for x in queries], axis=0)
    query = jnp.concatenate(split2(query), axis=0)
    new_keys, new_values = turn(key), value * root
    new_keys, new_values = [
        jnp.concatenate(pair, axis=0).astype(BF16)
        for pair in ((new_keys, new_values), (new_values, new_keys))
    ]
    tokens = keys_ref.shape[0]
    page = HD
    lane8 = iota((8, page), 1)
    chunk = 4 * page

    def score(keys):
        both = dot_t(query, keys)
        return both[:rows] + both[rows:]

    def mix(weights, values):
        both = dot(jnp.concatenate(split2(weights), axis=0), values)
        return both[:rows] + both[rows:]

    row = iota((rows, 16), 0) % 8
    col = iota((rows, 16), 1)
    new_ok = ((col < 8) & (col % 4 == row % 4) & (col // 4 <= row // 4)) & (
        limit_ref[0:1, page - 1 : page] > 0
    )
    new_scores = jnp.where(new_ok, score(new_keys), NEGATIVE)

    best = None
    for start in range(0, tokens, chunk):
        part = score(keys_ref[start : start + chunk, :])
        for k in range(chunk // page):
            p = start // page + k
            ok = lane8 < limit_ref[:, p : p + 1]
            piece = part[:, k * page : (k + 1) * page].reshape(rows // 8, 8, page)
            piece = jnp.where(ok[None], piece, NEGATIVE).reshape(rows, page)
            score_ref[:, start + k * page : start + (k + 1) * page] = piece
            best = piece if best is None else jnp.maximum(best, piece)
    top = jnp.maximum(
        jnp.max(best, axis=-1, keepdims=True), jnp.max(new_scores, axis=-1, keepdims=True)
    )
    top = jnp.maximum(top, FLOOR)
    new_weights = jnp.exp(new_scores - top)
    total = jnp.sum(new_weights, axis=-1, keepdims=True)
    mixed = mix(new_weights, new_values)
    sums = jnp.zeros((rows, page), F32)
    for start in range(0, tokens, chunk):
        weights = jnp.exp(score_ref[:, start : start + chunk] - top)
        for k in range(chunk // page):
            sums = sums + weights[:, k * page : (k + 1) * page]
        mixed = mixed + mix(weights, values_ref[start : start + chunk, :])
    total = total + jnp.sum(sums, axis=-1, keepdims=True)
    out_ref[0:rows, :] = mixed
    out_ref[rows : rows + 8, :] = tiled(top) + pltpu.roll(tiled(total), GROUP, 1)


STATS = 16
GROUP = 16


def tiled(columns):
    lane = iota((8, HD), 1)
    tile = jnp.zeros((8, HD), F32)
    for h in range(columns.shape[0] // 8):
        tile = jnp.where(lane == h, columns[8 * h : 8 * h + 8], tile)
    return tile


def post(mixed, top, total, out_ref):
    rows = mixed.shape[0]
    tile = jnp.zeros((8, HD), F32)
    for k, piece in enumerate(split3(top) + split3(total)):
        tile = tile + (pltpu.roll(piece, k * GROUP, 1) if k else piece)
    stats = jnp.concatenate([tile, jnp.zeros_like(tile)], axis=0).astype(BF16)
    mixed = mixed.astype(BF16)
    block = rows + STATS
    for k in range(out_ref.shape[0] // block):
        out_ref[k * block : k * block + rows, :] = mixed
        out_ref[k * block + rows : (k + 1) * block, :] = stats


def merge(parts_ref, rows, first=0, step=1):
    block = rows + STATS
    peers = range(first, parts_ref.shape[0] // block, step)
    tops, totals = [], []
    for k in peers:
        tile = parts_ref[k * block + rows : (k + 1) * block, :].astype(F32)[0:8]
        tile = tile + pltpu.roll(tile, HD - GROUP, 1) + pltpu.roll(tile, HD - 2 * GROUP, 1)
        tops.append(tile)
        totals.append(pltpu.roll(tile, HD - 3 * GROUP, 1))
    top = functools.reduce(jnp.maximum, tops)
    factors = [jnp.exp(x - top) for x in tops]
    total = sum(f * t for f, t in zip(factors, totals))
    mixed = []
    for g in range(rows // 16):
        acc = None
        for k, f in zip(peers, factors):
            part = parts_ref[k * block + 16 * g : k * block + 16 * g + 16, :].astype(F32)
            f = jnp.concatenate([f[:, 2 * g : 2 * g + 1], f[:, 2 * g + 1 : 2 * g + 2]], axis=0)
            acc = f * part if acc is None else acc + f * part
        mixed.append(acc)
    return mixed, top, total


def join_kernel(core_ref, rows_ref, out_ref):
    n = rows_ref.shape[0] // 2
    tops = [rows_ref[k * n + n - 8 : k * n + n, :] for k in range(2)]
    totals = [pltpu.roll(x, HD - GROUP, 1) for x in tops]
    top = jnp.maximum(tops[0], tops[1])
    factors = [jnp.exp(x - top) for x in tops]
    total = factors[0] * totals[0] + factors[1] * totals[1]
    mixed = [
        sum(
            factors[k][:, h : h + 1] * rows_ref[k * n + 8 * h : k * n + 8 * h + 8, :]
            for k in range(2)
        )
        for h in range(n // 8 - 1)
    ]
    live = iota((8, HD), 1) < GROUP // 2
    stats = []
    for x in (top, total):
        x = jnp.where(core_ref[0] == 0, x, pltpu.roll(x, HD - GROUP // 2, 1))
        stats.append(jnp.where(live, x, 0.0))
    post(jnp.concatenate(half(core_ref, mixed), axis=0), *stats, out_ref)


def merge_kernel(heads, parts_ref, out_ref):
    mixed, top, total = merge(parts_ref, 8 * heads)
    live = iota((8, HD), 1) < heads
    stats = [jnp.where(live, x, 0.0) for x in (top, total)]
    post(jnp.concatenate(mixed, axis=0), *stats, out_ref)


def output_kernel(heads, parts_ref, w_ref, out_ref):
    lhs = []
    for core in range(2):
        mixed, _, total = merge(parts_ref, 8 * heads, core, 2)
        inverse = 1.0 / jnp.where(iota((8, HD), 1) < heads, total, 1.0)
        for h in range(heads):
            row = mixed[h // 2][8 * (h % 2) : 8 * (h % 2) + 8]
            lhs.append(row * inverse[:, h : h + 1])
    lhs = jnp.concatenate(lhs, axis=1)
    part = dot(jnp.concatenate(split2(lhs), axis=0), w_ref[...])
    part = part[0:8] + part[8:16]
    for k in range(out_ref.shape[0] // 8):
        out_ref[k * 8 : (k + 1) * 8, :] = part


def deliver_kernel(owners_ref, parts_ref, out_ref):
    total = parts_ref[0:8, :]
    for k in range(1, parts_ref.shape[0] // 8):
        total = total + parts_ref[k * 8 : (k + 1) * 8, :]
    width = total.shape[1]
    out_ref[...] = jnp.zeros_like(out_ref)
    for b in range(4):
        pair = jnp.concatenate([total[b : b + 1], total[4 + b : 5 + b]], axis=0).astype(BF16)
        place = pl.multiple_of(owners_ref[b] * width, width)
        out_ref[:, pl.ds(place, width)] = pair


def body(hidden, norm_gain, w_query, w_keyval, w_out, cache, page_table, lengths, owners):
    n_steps, n_reqs, width_local = hidden.shape
    ctx, around = ("z", "x", "core"), ("x", "core")
    far, near = lax.axis_size("z"), lax.axis_size(around)
    peers = far * near
    groups = lax.axis_size("head")
    device_now = lax.axis_index(ctx)
    width_total = width_local * peers
    pages, page_len = cache.shape[0], cache.shape[1]
    vmem, hbm, smem = pltpu.VMEM, pl.ANY, pltpu.SMEM

    def exchange(x, axis, dim=0):
        return lax.all_to_all(x, axis, dim, dim, tiled=True)

    heads = w_query.shape[1] // HD
    coded, block = TILE * (heads // 4 + 2), 4 * heads + STATS
    core = lax.axis_index("core").astype(jnp.int32).reshape(1)

    with jax.named_scope("project"):
        chunks = 2
        parts = call(
            project_kernel,
            jax.ShapeDtypeStruct((8 * (heads + 3), HD), F32),
            [hbm] * 4,
            scratch=[
                pltpu.VMEM(hidden.shape, BF16),
                pltpu.VMEM(norm_gain.shape, BF16),
                pltpu.VMEM(w_query.shape, BF16),
                pltpu.VMEM(w_keyval.shape, BF16),
                pltpu.SemaphoreType.DMA((chunks + 3,)),
            ],
            limit=60,
        )(hidden, norm_gain, w_query, w_keyval)
    parts = lax.all_gather(parts, "core", axis=0, tiled=True)
    with jax.named_scope("pair"):
        parts = call(
            pair_kernel, jax.ShapeDtypeStruct((far * coded, HD), jnp.int16), [smem, vmem]
        )(core, parts)
    parts, lengths, page_table, cache = lax.optimization_barrier(
        (parts, lengths, page_table, cache)
    )
    parts = exchange(parts.reshape(far, coded, HD), "z").reshape(far * coded, HD)

    position = (lengths[None, :] + jnp.arange(n_steps, dtype=jnp.int32)[:, None]).astype(F32)
    angles = position.reshape(n_steps * n_reqs, 1) * frequencies(HD)
    cosine, sine = jnp.cos(angles), jnp.sin(angles)
    cosine = jnp.concatenate([cosine, cosine], axis=-1)
    sine = jnp.concatenate([-sine, sine], axis=-1)

    lane = np.arange(HD, dtype=np.int32)
    global_ids = jnp.where(lane < pages, device_now * pages + lane, -2)
    logical = np.arange(page_table.shape[1], dtype=np.int32)
    in_page = jnp.clip(lengths[:, None] - logical[None, :] * page_len, 0, page_len)
    limit = jnp.sum(
        jnp.where(page_table[:, :, None] == global_ids[None, None, :], in_page[:, :, None], 0),
        axis=1,
    )
    limit = limit + jnp.where(lane == HD - 1, (device_now == 0).astype(jnp.int32), 0)[None]
    limit = jnp.concatenate([limit, limit], axis=0)
    tokens = cache.reshape(pages * page_len, 2 * HD)
    keys, values = tokens[:, :HD], tokens[:, HD:]
    parts, cosine, sine, limit, keys, values = lax.optimization_barrier(
        (parts, cosine, sine, limit, keys, values)
    )

    with jax.named_scope("sum"):
        parts = call(
            functools.partial(sum_kernel, heads // 2),
            jax.ShapeDtypeStruct((near * coded, HD), jnp.int16),
            [vmem],
        )(parts)
    parts = exchange(parts.reshape(near, coded, HD), around).reshape(near * coded, HD)
    with jax.named_scope("attend"):
        parts = call(
            functools.partial(attend_kernel, HD ** (-0.5), 1.0 / width_total),
            jax.ShapeDtypeStruct((8 * heads + 8, HD), F32),
            [vmem] * 6,
            scratch=[pltpu.VMEM((8 * heads, pages * page_len), F32)],
        )(parts, cosine, sine, limit, keys, values)
    parts = lax.all_gather(parts, "core", axis=0, tiled=True)
    with jax.named_scope("join"):
        parts = call(
            join_kernel, jax.ShapeDtypeStruct((far * block, HD), BF16), [smem, vmem]
        )(core, parts)
    parts = exchange(parts.reshape(far, block, HD), "z").reshape(far * block, HD)
    with jax.named_scope("merge"):
        parts = call(
            functools.partial(merge_kernel, heads // 2),
            jax.ShapeDtypeStruct((near * block, HD), BF16),
            [vmem],
        )(parts)
    parts = exchange(parts.reshape(near, block, HD), around).reshape(near * block, HD)
    with jax.named_scope("output"):
        parts = call(
            functools.partial(output_kernel, heads // 2),
            jax.ShapeDtypeStruct((8 * groups, width_local), F32),
            [vmem] * 2,
        )(parts, w_out)
    parts = exchange(parts.reshape(groups, 8, width_local), "head")
    with jax.named_scope("deliver"):
        sent = call(
            deliver_kernel, jax.ShapeDtypeStruct((n_steps, width_total), BF16), [smem, vmem]
        )(owners, parts.reshape(8 * groups, width_local))
    return exchange(sent, ctx, 1)[None]


def solution(mesh):
    ctx = ("z", "x", "core")
    x, core = 4, 2
    split = Mesh(
        mesh.devices.reshape(mesh.shape["ctx"] // (x * core), x, core, mesh.shape["head"]),
        ("z", "x", "core", "head"),
    )
    placed = (
        P(None, None, ctx),
        P(ctx),
        P(ctx, "head"),
        P(ctx, "head"),
        P("head", ctx),
        P(ctx, None, "head", None),
        P(),
        P(),
        P(),
    )
    return jax.shard_map(
        body, mesh=split, in_specs=placed, out_specs=P(ctx, None, None), check_vma=False
    )
```
